32 devices in a mesh: groups: 1, dp: 32 (over z, y, x, core).
Axes of the slice: x: 2, y: 2, z: 4, core: 2. Of those that a mesh axis runs over, the one named last changes fastest.
Arguments:
- hidden_in: bfloat16 [256, 2, 1024], P(('groups', 'dp')), may hold values from -6 to 6
- query_in: bfloat16 [256, 2, 1024], P(('groups', 'dp')), may hold values from -6 to 6
- key_in: bfloat16 [256, 2, 1024], P(('groups', 'dp')), may hold values from -6 to 6
- value_in: bfloat16 [256, 2, 2048], P(('groups', 'dp')), may hold values from -6 to 6
- gate_in: bfloat16 [256, 2, 2048], P(('groups', 'dp')), may hold values from -6 to 6
- decay_in: bfloat16 [256, 2, 16], P(('groups', 'dp')), may hold values from -4 to 4
- beta_in: bfloat16 [256, 2, 16], P(('groups', 'dp')), may hold values from -5 to 5
- decay_log: float32 [16], replicated, may hold values from -3 to 2
- step_bias: float32 [16], replicated, may hold values from -1 to 1
- norm_gain: float32 [128], replicated, may hold values from 0.5 to 1.5
- state_in: bfloat16 [256, 16, 128, 128], P(('groups', 'dp')), may hold values from -3 to 3
- out_proj: bfloat16 [2048, 1024], replicated, may hold values from -0.125 to 0.125
- post_gain: float32 [1024], replicated, may hold values from 0.5 to 1.5
- router_weight: bfloat16 [1024, 32], replicated, may hold values from -0.1875 to 0.1875
- expert_gate_up: bfloat16 [32, 1024, 512], P('dp'), may hold values from -0.1875 to 0.1875
- expert_down: bfloat16 [32, 256, 1024], P('dp'), may hold values from -0.375 to 0.375
- expert_ids: int32 [256, 2, 10], P(('groups', 'dp')), may hold values from 0 to 31, all different within a row; in each aligned block of 16 rows (0 to 15, 16 to 31, ..., all dimensions but the last counted through in order) at most 8 rows name the same one
Outputs:
- layer_out: bfloat16 [256, 2, 1024], P(('groups', 'dp'))
The draws below stay inside these ranges and needn't reach their ends.
Inputs may be any that keep to these rules, and one draw needn't show every extreme that they name: `expert_ids`: each row and position names 10 different experts. Taking rows and positions in order, in each aligned block of 16 of them no expert is named more than 8 times, a bound that some block reaches.
All inputs are finite; a program needn't handle non-finite values.
Results may differ from the reference program's by a relative error of at most 0.0095.
Values may be sent and summed in bfloat16 or wider, within the bound.
No kernel may reach another device: no remote copies, remote signals or barrier semaphores. Data moves between devices by JAX's collectives and lax.ppermute only.
A program may use at most 64 MiB of HBM per device.

```python
import math
import jax
import jax.numpy as jnp
import numpy as np
from jax import lax

D = 1024
HK = 8
HV = 16
DK = 128
DV = 128
EFF = 256
TOP = 10
ROWS_DEV = 8
EXPERTS = 32
ROWS = 256
CAP = 8
N_DP = 32


def block_scale(rng, extent, cuts, low, largest):
    loudness = 1.0
    for axis_at, blocks in cuts:
        steps = jax.random.uniform(jax.random.fold_in(jax.random.fold_in(rng, 6), axis_at), (blocks,), jnp.float32, low / len(cuts), largest / len(cuts))
        loudness = loudness * jnp.repeat(jnp.exp(steps), extent[axis_at] // blocks).reshape((-1,) + (1,) * (len(extent) - 1 - axis_at))
    return loudness


def routed_block(rng, own, number, rows, amount, top, reach, lean):
    sequence = jax.random.permutation(rng, amount)
    packed, common = portions_of(amount, rows * top, reach, lean, True), portions_of(amount, rows * top, reach, lean, False)
    places = jnp.arange(amount)

    def named(tallies, offset_by):
        used = int((tallies > 0).sum())
        fixed = max(1, used // 4)
        moved = fixed + (places - fixed + offset_by * (used - fixed)) % max(1, amount - fixed)
        return jnp.zeros((amount,), jnp.int32).at[sequence[jnp.where(places < fixed, places, moved)]].set(jnp.asarray(tallies, jnp.int32))

    tallies = jnp.where(number % 4 == 0, named(packed, number // 4), named(common, number - number // 4 - 1))
    mixed = jax.random.permutation(jax.random.fold_in(own, 3), amount)
    giver, sink = mixed[0:amount // 2 * 2:2], mixed[1:amount // 2 * 2:2]
    slack = jnp.minimum(tallies[giver] - 1, reach - tallies[sink]) // 2
    slack = jnp.where((giver == sequence[0]) | (sink == sequence[0]) | (tallies[sink] == 0), 0, jnp.maximum(slack, 0))
    moved = jax.random.randint(jax.random.fold_in(own, 4), (amount // 2,), 0, 1 << 20) % (slack + 1)
    tallies = tallies.at[giver].add(-moved).at[sink].add(moved)
    members = jnp.searchsorted(jnp.cumsum(tallies), jnp.arange(rows * top), side="right").astype(jnp.int32)
    table = members.reshape(top, rows).T
    table = table[jax.random.permutation(jax.random.fold_in(own, 1), rows)]
    offset_by = jax.random.randint(jax.random.fold_in(own, 2), (rows, 1), 0, top)
    return jnp.take_along_axis(table, (jnp.arange(top)[None, :] + offset_by) % top, axis=1)


def portions_of(number_of, total, limit, skew, full):
    portions = [(1 << 20) // math.isqrt(standing ** skew) + 1 for standing in range(1, number_of + 1)]
    largest = limit if full else min(limit, max(-(-total // number_of), total * portions[0] // sum(portions)))
    least = 1 if total - largest >= number_of - 1 else 0
    given, surplus = [largest] + [least] * (number_of - 1), total - largest - least * (number_of - 1)
    while surplus > 0:
        candidates = [i for i in range(1, number_of) if given[i] < largest] or [i for i in range(1, number_of) if given[i] < limit]
        mass, budget = sum([portions[i] for i in candidates]), surplus
        for i in candidates:
            extra = min(limit - given[i], max(1, budget * portions[i] // mass), surplus)
            given[i] = given[i] + extra
            surplus = surplus - extra
    return np.array(given)


def centred(key, extent, deviation, reach, cuts=(), kind=jnp.bfloat16):
    drawn = deviation * jax.random.normal(key, extent, jnp.float32)
    if cuts:
        drawn = drawn * block_scale(key, extent, cuts, -0.22, 0.18)
    return jnp.clip(drawn, -reach, reach).astype(kind)


def setup_inputs(seed: int = 0, part: int = 0) -> dict:
    seeds = jax.random.split(jax.random.key(seed), 18)
    own_keys = jax.random.split(jax.random.fold_in(seeds[17], part), 18)
    hidden_in = centred(own_keys[0], (ROWS, 2, D), 1.0, 6.0, ((0, 32),))
    query_in = centred(own_keys[1], (ROWS, 2, HK * DK), 1.0, 6.0, ((0, 32),))
    key_in = centred(own_keys[2], (ROWS, 2, HK * DK), 1.0, 6.0, ((0, 32),))
    value_in = centred(own_keys[3], (ROWS, 2, HV * DV), 1.0, 6.0, ((0, 32),))
    gate_in = centred(own_keys[4], (ROWS, 2, HV * DV), 1.0, 6.0, ((0, 32),))
    decay_in = centred(own_keys[5], (ROWS, 2, HV), 1.0, 4.0, ((0, 32),))
    beta_in = centred(own_keys[6], (ROWS, 2, HV), 1.5, 5.0, ((0, 32),))
    decay_log = jnp.clip(jax.random.uniform(seeds[7], (HV,), jnp.float32, -3.0, 2.0), -3.0, 2.0)
    step_bias = jnp.clip(jax.random.uniform(seeds[8], (HV,), jnp.float32, -1.0, 1.0), -1.0, 1.0)
    norm_gain = jnp.clip(1.0 + 0.1 * jax.random.normal(seeds[9], (DV,), jnp.float32), 0.5, 1.5)
    state_in = centred(own_keys[10], (ROWS, HV, DK, DV), 0.5, 3.0, ((0, 32),))
    out_proj = centred(seeds[11], (HV * DV, D), (HV * DV) ** -0.5, 0.125)
    post_gain = jnp.clip(1.0 + 0.1 * jax.random.normal(seeds[12], (D,), jnp.float32), 0.5, 1.5)
    router_weight = centred(seeds[13], (D, EXPERTS), D ** -0.5, 0.1875)
    expert_gate_up = centred(seeds[14], (EXPERTS, D, 2 * EFF), D ** -0.5, 0.1875, ((0, 32),))
    expert_down = centred(seeds[15], (EXPERTS, EFF, D), EFF ** -0.5, 0.375, ((0, 32),))
    expert_ids_keys = jax.random.split(jax.random.fold_in(own_keys[16], 1), ROWS * 2 // (2 * ROWS_DEV))
    expert_ids_turns = jax.random.permutation(jax.random.fold_in(own_keys[16], 3), ROWS * 2 // (2 * ROWS_DEV))
    expert_ids = jax.vmap(lambda own, number: routed_block(jax.random.fold_in(own_keys[16], 2), own, number, 2 * ROWS_DEV, EXPERTS, TOP, CAP, 2))(expert_ids_keys, expert_ids_turns).reshape((ROWS, 2, TOP))
    return dict(hidden_in=hidden_in, query_in=query_in, key_in=key_in, value_in=value_in, gate_in=gate_in, decay_in=decay_in, beta_in=beta_in, decay_log=decay_log, step_bias=step_bias, norm_gain=norm_gain, state_in=state_in, out_proj=out_proj, post_gain=post_gain, router_weight=router_weight, expert_gate_up=expert_gate_up, expert_down=expert_down, expert_ids=expert_ids)


eps_norm = 1e-06

def delta_block(query_in, key_in, value_in, gate_in, decay_in, beta_in, state_in, decay_log, step_bias, norm_gain):
    row_count = query_in.shape[0]
    value_heads = state_in.shape[1]
    key_size = state_in.shape[2]
    value_size = state_in.shape[3]
    key_heads = query_in.shape[2] // key_size
    repeat_count = value_heads // key_heads
    query_all = query_in.astype(jnp.float32).reshape(row_count, 2, key_heads, key_size)
    query_all = query_all * lax.rsqrt(lax.optimization_barrier(jnp.sum(query_all * query_all, axis=-1, keepdims=True)) + eps_norm) * key_size ** (-0.5)
    key_all = key_in.astype(jnp.float32).reshape(row_count, 2, key_heads, key_size)
    key_all = key_all * lax.rsqrt(lax.optimization_barrier(jnp.sum(key_all * key_all, axis=-1, keepdims=True)) + eps_norm)
    query_all = jnp.repeat(query_all, repeat_count, axis=2)
    key_all = jnp.repeat(key_all, repeat_count, axis=2)
    value_all = value_in.astype(jnp.float32).reshape(row_count, 2, value_heads, value_size)
    gate_all = gate_in.astype(jnp.float32).reshape(row_count, 2, value_heads, value_size)
    decay_rate = jnp.exp(-jnp.exp(decay_log) * jax.nn.softplus(decay_in.astype(jnp.float32) + step_bias))
    beta_gate = jax.nn.sigmoid(beta_in.astype(jnp.float32))
    memory = state_in.astype(jnp.float32)
    outputs = []
    for position in range(2):
        keys_now = key_all[:, position]
        memory = memory * decay_rate[:, position, :, None, None]
        recalled = lax.optimization_barrier(jnp.sum(memory * keys_now[..., None], axis=2))
        update = beta_gate[:, position, :, None] * (value_all[:, position] - recalled)
        memory = memory + keys_now[..., None] * update[:, :, None, :]
        outputs.append(lax.optimization_barrier(jnp.sum(memory * query_all[:, position][..., None], axis=2)))
    core_out = jnp.stack(outputs, axis=1)
    scaled = core_out * lax.rsqrt(lax.optimization_barrier(jnp.mean(core_out * core_out, axis=-1, keepdims=True)) + eps_norm) * norm_gain * jax.nn.silu(gate_all)
    return scaled.reshape(row_count, 2, value_heads * value_size).astype(jnp.bfloat16)

def gate_weights(logits_all, picked_ids):
    expert_index = jnp.arange(logits_all.shape[1], dtype=jnp.int32)
    chosen = lax.optimization_barrier(jnp.sum(jnp.where(picked_ids[:, :, None] == expert_index, logits_all[:, None, :], 0.0), axis=-1))
    raised = jnp.exp(chosen)
    return raised / lax.optimization_barrier(jnp.sum(raised, axis=-1, keepdims=True))

def slot_numbers(picked_flat):
    pick_total = picked_flat.shape[0]
    pick_order = jnp.arange(pick_total, dtype=jnp.int32)
    earlier_same = (picked_flat[:, None] == picked_flat[None, :]) & (pick_order[:, None] > pick_order[None, :])
    return lax.optimization_barrier(jnp.sum(earlier_same.astype(jnp.int32), axis=1))

def reference(hidden_in, query_in, key_in, value_in, gate_in, decay_in, beta_in, decay_log, step_bias, norm_gain, state_in, out_proj, post_gain, router_weight, expert_gate_up, expert_down, expert_ids):

    def split_rows(whole_array):
        return whole_array.reshape((N_DP, ROWS_DEV) + whole_array.shape[1:])

    def one_block(pieces):
        return delta_block(pieces[0], pieces[1], pieces[2], pieces[3], pieces[4], pieces[5], pieces[6], decay_log, step_bias, norm_gain)
    mixer_out = lax.map(one_block, (split_rows(query_in), split_rows(key_in), split_rows(value_in), split_rows(gate_in), split_rows(decay_in), split_rows(beta_in), split_rows(state_in)))
    token_count = ROWS * 2
    mixer_out = mixer_out.reshape(token_count, HV * DV)
    residual = hidden_in.astype(jnp.float32).reshape(token_count, D)
    middle = (residual + jnp.dot(mixer_out, out_proj, preferred_element_type=jnp.float32)).astype(jnp.bfloat16)
    middle_wide = middle.astype(jnp.float32)
    routed = (middle_wide * lax.rsqrt(lax.optimization_barrier(jnp.mean(middle_wide * middle_wide, axis=-1, keepdims=True)) + eps_norm) * post_gain).astype(jnp.bfloat16)
    logits_all = jnp.dot(routed, router_weight, preferred_element_type=jnp.float32)
    picked_ids = expert_ids.reshape(token_count, TOP)
    gate_share = gate_weights(logits_all, picked_ids)
    block_picks = picked_ids.reshape(N_DP, 2 * ROWS_DEV * TOP)
    slot_number = jax.vmap(slot_numbers)(block_picks).reshape(token_count, TOP)
    token_block = (jnp.arange(token_count, dtype=jnp.int32) // (2 * ROWS_DEV))[:, None]
    destination = ((picked_ids * N_DP + token_block) * CAP + slot_number).reshape(-1)
    buffer = jnp.zeros((EXPERTS * N_DP * CAP, D), jnp.bfloat16).at[destination].set(jnp.repeat(routed, TOP, axis=0))
    block_rows = buffer.reshape(EXPERTS, N_DP * CAP, D)

    def expert_apply(expert_item):
        both_parts = jnp.dot(expert_item[0], expert_item[1], preferred_element_type=jnp.float32)
        activated = (jax.nn.silu(both_parts[:, :EFF]) * both_parts[:, EFF:]).astype(jnp.bfloat16)
        return jnp.dot(activated, expert_item[2], preferred_element_type=jnp.float32).astype(jnp.bfloat16)
    results = lax.map(expert_apply, (block_rows, expert_gate_up, expert_down))
    picked = results.reshape(EXPERTS * N_DP * CAP, D)[destination].reshape(token_count, TOP, D)
    mixture = lax.optimization_barrier(jnp.sum(gate_share[:, :, None] * picked.astype(jnp.float32), axis=1))
    return (middle_wide + mixture).astype(jnp.bfloat16).reshape(ROWS, 2, D)
```

```python
import functools

import jax
import jax.numpy as jnp
from jax import lax
from jax.experimental import pallas as pl
from jax.experimental.pallas import tpu as pltpu
from jax.sharding import PartitionSpec as P

eps_norm = 1e-06
f32 = jnp.float32
bf16 = jnp.bfloat16


def split_two(x):
    high = x.astype(bf16)
    low = (x - high.astype(f32)).astype(bf16)
    return high, low


def nt_dot(a, b):
    return lax.dot_general(a, b, (((1,), (1,)), ((), ())), preferred_element_type=f32)


def mixer_kernel(
    capacity,
    hidden_ref,
    query_ref,
    key_ref,
    value_ref,
    gate_ref,
    decay_in_ref,
    beta_in_ref,
    decay_log_ref,
    step_bias_ref,
    norm_gain_ref,
    post_gain_ref,
    router_ref,
    ids_ref,
    state_hbm,
    proj_hbm,
    blocks_ref,
    weights_ref,
    middle_ref,
    state_buf,
    proj_buf,
    left_buf,
    right_buf,
    state_sem,
    proj_sem,
):
    rows = query_ref.shape[0]
    value_heads, key_size, value_size = state_hbm.shape[1:]
    key_heads = query_ref.shape[2] // key_size
    share = value_heads // key_heads
    span = share * value_size
    chunks = proj_sem.shape[0]
    depth = proj_hbm.shape[0] // chunks

    def state_copy(h):
        return pltpu.make_async_copy(
            state_hbm.at[:, pl.ds(h * share, share)], state_buf.at[h], state_sem.at[h]
        )

    def proj_copy(c):
        part = pl.ds(c * depth, depth)
        return pltpu.make_async_copy(proj_hbm.at[part], proj_buf.at[part], proj_sem.at[c])

    for h in range(key_heads):
        state_copy(h).start()
    for c in range(chunks):
        proj_copy(c).start()

    query_all = query_ref[...].astype(f32)
    key_all = key_ref[...].astype(f32)
    value_all = value_ref[...].astype(f32)
    gate_all = gate_ref[...].astype(f32)
    decay_in = decay_in_ref[...].astype(f32)
    beta_in = beta_in_ref[...].astype(f32)
    rate = -jnp.exp(decay_log_ref[...].reshape(1, value_heads))
    bias = step_bias_ref[...].reshape(1, value_heads)
    decays, betas = [], []
    for p in range(2):
        decays.append(jnp.exp(rate * jax.nn.softplus(decay_in[:, p, :] + bias)))
        betas.append(1.0 / (1.0 + jnp.exp(-beta_in[:, p, :])))
    gain = norm_gain_ref[...].reshape(1, value_size)

    mixed = [[], []]
    for h in range(key_heads):
        lanes = slice(h * key_size, (h + 1) * key_size)
        keys, queries = [], []
        for p in range(2):
            k = key_all[:, p, lanes]
            q = query_all[:, p, lanes]
            keys.append(k * lax.rsqrt(jnp.sum(k * k, axis=-1, keepdims=True) + eps_norm))
            queries.append(
                q
                * lax.rsqrt(jnp.sum(q * q, axis=-1, keepdims=True) + eps_norm)
                * key_size ** (-0.5)
            )
        vectors = (keys[0], queries[0], keys[1], queries[1])
        for j, v in enumerate(vectors):
            high = v.astype(bf16).astype(f32)
            left_buf[h, pl.ds(2 * j, rows, stride=8), :] = high
            left_buf[h, pl.ds(2 * j + 1, rows, stride=8), :] = v - high
        key_key = jnp.sum(keys[0] * keys[1], axis=-1, keepdims=True)
        key_query00 = jnp.sum(keys[0] * queries[0], axis=-1, keepdims=True)
        key_query01 = jnp.sum(keys[0] * queries[1], axis=-1, keepdims=True)
        key_query11 = jnp.sum(keys[1] * queries[1], axis=-1, keepdims=True)

        state_copy(h).wait()
        for r in range(rows):
            left = left_buf[h, r * 8 : (r + 1) * 8, :].astype(bf16)
            right = jnp.concatenate([state_buf[h, r, i] for i in range(share)], axis=-1)
            out = jnp.dot(left, right, preferred_element_type=f32)
            for i in range(share):
                right_buf[h, i, r * 8 : (r + 1) * 8, :] = out[:, i * value_size : (i + 1) * value_size]

        for i in range(share):
            n = h * share + i
            heads = slice(n * value_size, (n + 1) * value_size)
            part = [
                right_buf[h, i, pl.ds(2 * j, rows, stride=8), :]
                + right_buf[h, i, pl.ds(2 * j + 1, rows, stride=8), :]
                for j in range(4)
            ]
            d0, d1 = decays[0][:, n : n + 1], decays[1][:, n : n + 1]
            b0, b1 = betas[0][:, n : n + 1], betas[1][:, n : n + 1]
            u0 = b0 * (value_all[:, 0, heads] - d0 * part[0])
            o0 = d0 * part[1] + key_query00 * u0
            u1 = b1 * (value_all[:, 1, heads] - d1 * (d0 * part[2] + key_key * u0))
            o1 = d1 * (d0 * part[3] + key_query01 * u0) + key_query11 * u1
            for p, o in enumerate((o0, o1)):
                g = gate_all[:, p, heads]
                mean = jnp.mean(o * o, axis=-1, keepdims=True)
                mixed[p].append(
                    o * lax.rsqrt(mean + eps_norm) * gain * (g / (1.0 + jnp.exp(-g)))
                )

    mixer_out = jnp.concatenate(
        [jnp.concatenate(mixed[p], axis=-1) for p in range(2)], axis=0
    ).astype(bf16)
    hidden = hidden_ref[...].astype(f32)
    total = jnp.concatenate([hidden[:, p, :] for p in range(2)], axis=0)
    for c in range(chunks):
        proj_copy(c).wait()
        part = slice(c * depth, (c + 1) * depth)
        total = total + jnp.dot(mixer_out[:, part], proj_buf[part, :], preferred_element_type=f32)
    middle = total.astype(bf16)
    middle_ref[...] = middle
    wide = middle.astype(f32)
    routed = (
        wide
        * lax.rsqrt(jnp.mean(wide * wide, axis=-1, keepdims=True) + eps_norm)
        * post_gain_ref[...].reshape(1, wide.shape[1])
    ).astype(bf16)
    logits = jnp.dot(routed, router_ref[...], preferred_element_type=f32)

    tokens = 2 * rows
    experts = logits.shape[1]
    slots = experts * capacity
    ids = jnp.concatenate([ids_ref[:, p, :] for p in range(2)], axis=0)
    expert = lax.broadcasted_iota(jnp.int32, (tokens, experts), 1)
    chosen = jnp.zeros((tokens, experts), f32)
    for k in range(ids.shape[1]):
        chosen = chosen + (ids[:, k : k + 1] == expert).astype(f32)
    raised = jnp.where(chosen > 0.0, jnp.exp(logits), 0.0)
    share_all = raised / jnp.sum(raised, axis=-1, keepdims=True)
    later = lax.broadcasted_iota(jnp.int32, (tokens, tokens), 0)
    earlier = lax.broadcasted_iota(jnp.int32, (tokens, tokens), 1)
    below = (later > earlier).astype(bf16)
    chosen16 = chosen.astype(bf16)
    slot = jnp.dot(below, chosen16, preferred_element_type=f32)
    place = jnp.where(chosen > 0.0, slot, -1.0).astype(bf16)
    slot_expert = lax.broadcasted_iota(jnp.int32, (slots, experts), 0) // capacity
    spread = (slot_expert == lax.broadcasted_iota(jnp.int32, (slots, experts), 1)).astype(bf16)
    number = lax.broadcasted_iota(jnp.int32, (slots, tokens), 0)
    take = (nt_dot(spread, place) == (number % capacity).astype(f32)).astype(bf16)
    blocks_ref[...] = jnp.dot(take, routed, preferred_element_type=f32).astype(bf16)
    lane = lax.broadcasted_iota(jnp.int32, (tokens, slots), 1)
    match = nt_dot(place, spread) == (lane % capacity).astype(f32)
    high, low = split_two(share_all)
    spread_share = nt_dot(high, spread) + nt_dot(low, spread)
    weights_ref[...] = jnp.where(match, spread_share, 0.0)


def expert_kernel(blocks_ref, up_ref, down_ref, out_ref):
    hidden_units = down_ref.shape[1]
    both = jnp.dot(blocks_ref[...], up_ref[0], preferred_element_type=f32)
    g = both[:, :hidden_units]
    activated = (g / (1.0 + jnp.exp(-g)) * both[:, hidden_units:]).astype(bf16)
    out_ref[...] = jnp.dot(activated, down_ref[0], preferred_element_type=f32).astype(bf16)


def combine_kernel(returned_ref, weights_ref, middle_ref, out_ref):
    rows = out_ref.shape[0]
    high, low = split_two(weights_ref[...])
    returned = returned_ref[...]
    total = (
        middle_ref[...].astype(f32)
        + jnp.dot(high, returned, preferred_element_type=f32)
        + jnp.dot(low, returned, preferred_element_type=f32)
    ).astype(bf16)
    for p in range(2):
        out_ref[:, p, :] = total[p * rows : (p + 1) * rows]


def vmem(count):
    return [pl.BlockSpec(memory_space=pltpu.VMEM)] * count


def shards(
    hidden_in,
    query_in,
    key_in,
    value_in,
    gate_in,
    decay_in,
    beta_in,
    decay_log,
    step_bias,
    norm_gain,
    state_in,
    out_proj,
    post_gain,
    router_weight,
    expert_gate_up,
    expert_down,
    expert_ids,
):
    device_count = lax.axis_size("dp")
    expert_total = expert_gate_up.shape[0] * device_count
    row_count, _, model_width = hidden_in.shape
    pick_count = expert_ids.shape[2]
    value_heads, key_size, value_size = state_in.shape[1:]
    key_heads = query_in.shape[2] // key_size
    share = value_heads // key_heads
    token_count = row_count * 2
    capacity = min(
        token_count, max(2, (3 * row_count * pick_count + expert_total - 1) // expert_total)
    )
    slots = expert_total * capacity
    chunks = 4
    params = pltpu.CompilerParams(vmem_limit_bytes=48 * 1024 * 1024)
    blocks, weights, middle = pl.pallas_call(
        functools.partial(mixer_kernel, capacity),
        out_shape=(
            jax.ShapeDtypeStruct((slots, model_width), bf16),
            jax.ShapeDtypeStruct((token_count, slots), f32),
            jax.ShapeDtypeStruct((token_count, model_width), bf16),
        ),
        in_specs=vmem(13) + [pl.BlockSpec(memory_space=pl.ANY)] * 2,
        out_specs=tuple(vmem(3)),
        scratch_shapes=[
            pltpu.VMEM((key_heads, row_count, share, key_size, value_size), bf16),
            pltpu.VMEM(out_proj.shape, bf16),
            pltpu.VMEM((key_heads, 8 * row_count, key_size), f32),
            pltpu.VMEM((key_heads, share, 8 * row_count, value_size), f32),
            pltpu.SemaphoreType.DMA((key_heads,)),
            pltpu.SemaphoreType.DMA((chunks,)),
        ],
        compiler_params=params,
        name="mixer",
    )(
        hidden_in,
        query_in,
        key_in,
        value_in,
        gate_in,
        decay_in,
        beta_in,
        decay_log,
        step_bias,
        norm_gain,
        post_gain,
        router_weight,
        expert_ids,
        state_in,
        out_proj,
    )
    received = lax.all_to_all(blocks, "dp", split_axis=0, concat_axis=0, tiled=True)
    produced = pl.pallas_call(
        expert_kernel,
        out_shape=jax.ShapeDtypeStruct((slots, model_width), bf16),
        in_specs=vmem(3),
        out_specs=vmem(1)[0],
        compiler_params=params,
        name="experts",
    )(received, expert_gate_up, expert_down)
    returned = lax.all_to_all(produced, "dp", split_axis=0, concat_axis=0, tiled=True)
    return pl.pallas_call(
        combine_kernel,
        out_shape=jax.ShapeDtypeStruct(hidden_in.shape, bf16),
        in_specs=vmem(3),
        out_specs=vmem(1)[0],
        compiler_params=params,
        name="combine",
    )(returned, weights, middle)


def solution(mesh):
    rows = P(("groups", "dp"))
    placed = (
        (rows,) * 7 + (P(),) * 3 + (rows,) + (P(),) * 3 + (P("dp"),) * 2 + (rows,)
    )
    return jax.shard_map(
        shards,
        mesh=mesh,
        in_specs=placed,
        out_specs=rows,
        check_vma=False,
    )
```

```python
import functools

import jax
import jax.numpy as jnp
from jax import lax
from jax.experimental import pallas as pl
from jax.experimental.pallas import tpu as pltpu
from jax.sharding import PartitionSpec as P

eps_norm = 1e-06
f32 = jnp.float32
bf16 = jnp.bfloat16


def split_two(x):
    high = x.astype(bf16)
    low = (x - high.astype(f32)).astype(bf16)
    return high, low


def nt_dot(a, b):
    return lax.dot_general(a, b, (((1,), (1,)), ((), ())), preferred_element_type=f32)


def mixer_kernel(
    capacity,
    hidden_hbm,
    query_hbm,
    key_hbm,
    value_hbm,
    gate_hbm,
    decay_in_hbm,
    beta_in_hbm,
    decay_log_hbm,
    step_bias_hbm,
    norm_gain_hbm,
    post_gain_hbm,
    router_hbm,
    ids_hbm,
    state_hbm,
    proj_hbm,
    blocks_ref,
    weights_ref,
    middle_ref,
    hidden_ref,
    query_ref,
    key_ref,
    value_ref,
    gate_ref,
    decay_in_ref,
    beta_in_ref,
    decay_log_ref,
    step_bias_ref,
    norm_gain_ref,
    post_gain_ref,
    router_ref,
    ids_ref,
    state_buf,
    proj_buf,
    left_buf,
    right_buf,
    small_sem,
    state_sem,
    proj_sem,
):
    rows = query_ref.shape[0]
    value_heads, key_size, value_size = state_hbm.shape[1:]
    key_heads = query_ref.shape[2] // key_size
    share = value_heads // key_heads
    span = share * value_size
    chunks = proj_sem.shape[0]
    depth = proj_hbm.shape[0] // chunks

    def state_copy(h):
        return pltpu.make_async_copy(
            state_hbm.at[:, pl.ds(h * share, share)], state_buf.at[h], state_sem.at[h]
        )

    def proj_copy(c):
        part = pl.ds(c * depth, depth)
        return pltpu.make_async_copy(proj_hbm.at[part], proj_buf.at[part], proj_sem.at[c])

    pairs = (
        (key_hbm, key_ref),
        (query_hbm, query_ref),
        (decay_log_hbm, decay_log_ref),
        (step_bias_hbm, step_bias_ref),
        (decay_in_hbm, decay_in_ref),
        (beta_in_hbm, beta_in_ref),
        (norm_gain_hbm, norm_gain_ref),
        (value_hbm, value_ref),
        (gate_hbm, gate_ref),
        (ids_hbm, ids_ref),
        (hidden_hbm, hidden_ref),
        (post_gain_hbm, post_gain_ref),
        (router_hbm, router_ref),
    )
    small = [pltpu.make_async_copy(a, b, small_sem.at[i]) for i, (a, b) in enumerate(pairs)]
    early, late = small[:9], small[9:]
    for copy in early[:2]:
        copy.start()
    state_copy(0).start()
    for copy in early[2:]:
        copy.start()
    for h in range(1, key_heads):
        state_copy(h).start()
    for c in range(chunks):
        proj_copy(c).start()
    for copy in late:
        copy.start()
    for copy in early:
        copy.wait()

    query_all = query_ref[...].astype(f32)
    key_all = key_ref[...].astype(f32)
    value_all = value_ref[...].astype(f32)
    gate_all = gate_ref[...].astype(f32)
    decay_in = decay_in_ref[...].astype(f32)
    beta_in = beta_in_ref[...].astype(f32)
    rate = -jnp.exp(decay_log_ref[...].reshape(1, value_heads))
    bias = step_bias_ref[...].reshape(1, value_heads)
    decays, betas = [], []
    for p in range(2):
        decays.append(jnp.exp(rate * jax.nn.softplus(decay_in[:, p, :] + bias)))
        betas.append(1.0 / (1.0 + jnp.exp(-beta_in[:, p, :])))
    gain = norm_gain_ref[...].reshape(1, value_size)

    mixed = [[], []]
    for h in range(key_heads):
        lanes = slice(h * key_size, (h + 1) * key_size)
        keys, queries = [], []
        for p in range(2):
            k = key_all[:, p, lanes]
            q = query_all[:, p, lanes]
            keys.append(k * lax.rsqrt(jnp.sum(k * k, axis=-1, keepdims=True) + eps_norm))
            queries.append(
                q
                * lax.rsqrt(jnp.sum(q * q, axis=-1, keepdims=True) + eps_norm)
                * key_size ** (-0.5)
            )
        vectors = (keys[0], queries[0], keys[1], queries[1])
        for j, v in enumerate(vectors):
            high = v.astype(bf16).astype(f32)
            left_buf[h, pl.ds(2 * j, rows, stride=8), :] = high
            left_buf[h, pl.ds(2 * j + 1, rows, stride=8), :] = v - high
        key_key = jnp.sum(keys[0] * keys[1], axis=-1, keepdims=True)
        key_query00 = jnp.sum(keys[0] * queries[0], axis=-1, keepdims=True)
        key_query01 = jnp.sum(keys[0] * queries[1], axis=-1, keepdims=True)
        key_query11 = jnp.sum(keys[1] * queries[1], axis=-1, keepdims=True)

        state_copy(h).wait()
        for r in range(rows):
            left = left_buf[h, r * 8 : (r + 1) * 8, :].astype(bf16)
            right = jnp.concatenate([state_buf[h, r, i] for i in range(share)], axis=-1)
            out = jnp.dot(left, right, preferred_element_type=f32)
            for i in range(share):
                right_buf[h, i, r * 8 : (r + 1) * 8, :] = out[:, i * value_size : (i + 1) * value_size]

        for i in range(share):
            n = h * share + i
            heads = slice(n * value_size, (n + 1) * value_size)
            part = [
                right_buf[h, i, pl.ds(2 * j, rows, stride=8), :]
                + right_buf[h, i, pl.ds(2 * j + 1, rows, stride=8), :]
                for j in range(4)
            ]
            d0, d1 = decays[0][:, n : n + 1], decays[1][:, n : n + 1]
            b0, b1 = betas[0][:, n : n + 1], betas[1][:, n : n + 1]
            u0 = b0 * (value_all[:, 0, heads] - d0 * part[0])
            o0 = d0 * part[1] + key_query00 * u0
            u1 = b1 * (value_all[:, 1, heads] - d1 * (d0 * part[2] + key_key * u0))
            o1 = d1 * (d0 * part[3] + key_query01 * u0) + key_query11 * u1
            for p, o in enumerate((o0, o1)):
                g = gate_all[:, p, heads]
                mean = jnp.mean(o * o, axis=-1, keepdims=True)
                mixed[p].append(
                    o * lax.rsqrt(mean + eps_norm) * gain * (g / (1.0 + jnp.exp(-g)))
                )

    mixer_out = jnp.concatenate(
        [jnp.concatenate(mixed[p], axis=-1) for p in range(2)], axis=0
    ).astype(bf16)
    for copy in late:
        copy.wait()
    hidden = hidden_ref[...].astype(f32)
    total = jnp.concatenate([hidden[:, p, :] for p in range(2)], axis=0)
    for c in range(chunks):
        proj_copy(c).wait()
        part = slice(c * depth, (c + 1) * depth)
        total = total + jnp.dot(mixer_out[:, part], proj_buf[part, :], preferred_element_type=f32)
    middle = total.astype(bf16)
    middle_ref[...] = middle
    wide = middle.astype(f32)
    routed = (
        wide
        * lax.rsqrt(jnp.mean(wide * wide, axis=-1, keepdims=True) + eps_norm)
        * post_gain_ref[...].reshape(1, wide.shape[1])
    ).astype(bf16)
    logits = nt_dot(routed, router_ref[...])

    tokens = 2 * rows
    experts = logits.shape[1]
    slots = experts * capacity
    ids = jnp.concatenate([ids_ref[:, p, :] for p in range(2)], axis=0)
    expert = lax.broadcasted_iota(jnp.int32, (tokens, experts), 1)
    chosen = jnp.zeros((tokens, experts), f32)
    for k in range(ids.shape[1]):
        chosen = chosen + (ids[:, k : k + 1] == expert).astype(f32)
    raised = jnp.where(chosen > 0.0, jnp.exp(logits), 0.0)
    share_all = raised / jnp.sum(raised, axis=-1, keepdims=True)
    later = lax.broadcasted_iota(jnp.int32, (tokens, tokens), 0)
    earlier = lax.broadcasted_iota(jnp.int32, (tokens, tokens), 1)
    below = (later > earlier).astype(bf16)
    chosen16 = chosen.astype(bf16)
    slot = jnp.dot(below, chosen16, preferred_element_type=f32)
    place = jnp.where(chosen > 0.0, slot, -1.0).astype(bf16)
    slot_expert = lax.broadcasted_iota(jnp.int32, (slots, experts), 0) // capacity
    spread = (slot_expert == lax.broadcasted_iota(jnp.int32, (slots, experts), 1)).astype(bf16)
    number = lax.broadcasted_iota(jnp.int32, (slots, tokens), 0)
    take = (nt_dot(spread, place) == (number % capacity).astype(f32)).astype(bf16)
    blocks_ref[...] = jnp.dot(take, routed, preferred_element_type=f32).astype(bf16)
    lane = lax.broadcasted_iota(jnp.int32, (tokens, slots), 1)
    match = nt_dot(place, spread) == (lane % capacity).astype(f32)
    high, low = split_two(share_all)
    spread_share = nt_dot(high, spread) + nt_dot(low, spread)
    weights_ref[...] = jnp.where(match, spread_share, 0.0)


def expert_kernel(blocks_ref, up_ref, down_ref, out_ref):
    hidden_units = down_ref.shape[1]
    both = jnp.dot(blocks_ref[...], up_ref[0], preferred_element_type=f32)
    g = both[:, :hidden_units]
    activated = (g / (1.0 + jnp.exp(-g)) * both[:, hidden_units:]).astype(bf16)
    out_ref[...] = jnp.dot(activated, down_ref[0], preferred_element_type=f32).astype(bf16)


def combine_kernel(returned_ref, weights_ref, middle_ref, out_ref):
    rows = out_ref.shape[0]
    high, low = split_two(weights_ref[...])
    returned = returned_ref[...]
    total = (
        middle_ref[...].astype(f32)
        + jnp.dot(high, returned, preferred_element_type=f32)
        + jnp.dot(low, returned, preferred_element_type=f32)
    ).astype(bf16)
    for p in range(2):
        out_ref[:, p, :] = total[p * rows : (p + 1) * rows]


def vmem(count):
    return [pl.BlockSpec(memory_space=pltpu.VMEM)] * count


def shards(
    hidden_in,
    query_in,
    key_in,
    value_in,
    gate_in,
    decay_in,
    beta_in,
    decay_log,
    step_bias,
    norm_gain,
    state_in,
    out_proj,
    post_gain,
    router_weight,
    expert_gate_up,
    expert_down,
    expert_ids,
):
    device_count = lax.axis_size("dp")
    expert_total = expert_gate_up.shape[0] * device_count
    row_count, _, model_width = hidden_in.shape
    pick_count = expert_ids.shape[2]
    value_heads, key_size, value_size = state_in.shape[1:]
    key_heads = query_in.shape[2] // key_size
    share = value_heads // key_heads
    token_count = row_count * 2
    capacity = min(
        token_count, max(2, (3 * row_count * pick_count + expert_total - 1) // expert_total)
    )
    slots = expert_total * capacity
    chunks = 4
    params = pltpu.CompilerParams(vmem_limit_bytes=48 * 1024 * 1024)
    operands = (
        hidden_in,
        query_in,
        key_in,
        value_in,
        gate_in,
        decay_in,
        beta_in,
        decay_log,
        step_bias,
        norm_gain,
        post_gain,
        router_weight.T,
        expert_ids,
        state_in,
        out_proj,
    )
    operands = [pltpu.with_memory_space_constraint(x, pltpu.HBM) for x in operands]
    blocks, weights, middle = pl.pallas_call(
        functools.partial(mixer_kernel, capacity),
        out_shape=(
            jax.ShapeDtypeStruct((slots, model_width), bf16),
            jax.ShapeDtypeStruct((token_count, slots), f32),
            jax.ShapeDtypeStruct((token_count, model_width), bf16),
        ),
        in_specs=[pl.BlockSpec(memory_space=pltpu.HBM)] * len(operands),
        out_specs=tuple(vmem(3)),
        scratch_shapes=[pltpu.VMEM(x.shape, x.dtype) for x in operands[:13]]
        + [
            pltpu.VMEM((key_heads, row_count, share, key_size, value_size), bf16),
            pltpu.VMEM(out_proj.shape, bf16),
            pltpu.VMEM((key_heads, 8 * row_count, key_size), f32),
            pltpu.VMEM((key_heads, share, 8 * row_count, value_size), f32),
            pltpu.SemaphoreType.DMA((13,)),
            pltpu.SemaphoreType.DMA((key_heads,)),
            pltpu.SemaphoreType.DMA((chunks,)),
        ],
        compiler_params=params,
        name="mixer",
    )(*operands)
    received = lax.all_to_all(blocks, "dp", split_axis=0, concat_axis=0, tiled=True)
    produced = pl.pallas_call(
        expert_kernel,
        out_shape=jax.ShapeDtypeStruct((slots, model_width), bf16),
        in_specs=vmem(3),
        out_specs=vmem(1)[0],
        compiler_params=params,
        name="experts",
    )(received, expert_gate_up, expert_down)
    returned = lax.all_to_all(produced, "dp", split_axis=0, concat_axis=0, tiled=True)
    return pl.pallas_call(
        combine_kernel,
        out_shape=jax.ShapeDtypeStruct(hidden_in.shape, bf16),
        in_specs=vmem(3),
        out_specs=vmem(1)[0],
        compiler_params=params,
        name="combine",
    )(returned, weights, middle)


def solution(mesh):
    rows = P(("groups", "dp"))
    placed = (
        (rows,) * 7 + (P(),) * 3 + (rows,) + (P(),) * 3 + (P("dp"),) * 2 + (rows,)
    )
    return jax.shard_map(
        shards,
        mesh=mesh,
        in_specs=placed,
        out_specs=rows,
        check_vma=False,
    )
```

```python
import functools

import jax
import jax.numpy as jnp
from jax import lax
from jax.experimental import pallas as pl
from jax.experimental.pallas import tpu as pltpu
from jax.sharding import PartitionSpec as P

eps_norm = 1e-06
f32 = jnp.float32
bf16 = jnp.bfloat16


def split_two(x):
    high = x.astype(bf16)
    low = (x - high.astype(f32)).astype(bf16)
    return high, low


def nt_dot(a, b):
    return lax.dot_general(a, b, (((1,), (1,)), ((), ())), preferred_element_type=f32)


def mixer_kernel(
    hidden_hbm,
    query_hbm,
    key_hbm,
    value_hbm,
    gate_hbm,
    decay_in_hbm,
    beta_in_hbm,
    decay_log_hbm,
    step_bias_hbm,
    norm_gain_hbm,
    post_gain_hbm,
    router_hbm,
    ids_hbm,
    state_hbm,
    proj_hbm,
    routed_ref,
    middle_ref,
    hidden_ref,
    query_ref,
    key_ref,
    value_ref,
    gate_ref,
    decay_in_ref,
    beta_in_ref,
    decay_log_ref,
    step_bias_ref,
    norm_gain_ref,
    post_gain_ref,
    router_ref,
    ids_ref,
    state_buf,
    proj_buf,
    left_buf,
    right_buf,
    small_sem,
    state_sem,
    proj_sem,
):
    rows = query_ref.shape[0]
    value_heads, key_size, value_size = state_hbm.shape[1:]
    key_heads = query_ref.shape[2] // key_size
    share = value_heads // key_heads
    span = share * value_size
    chunks = proj_sem.shape[0]
    depth = proj_hbm.shape[0] // chunks

    def state_copy(h):
        return pltpu.make_async_copy(
            state_hbm.at[:, pl.ds(h * share, share)], state_buf.at[h], state_sem.at[h]
        )

    def proj_copy(c):
        part = pl.ds(c * depth, depth)
        return pltpu.make_async_copy(proj_hbm.at[part], proj_buf.at[part], proj_sem.at[c])

    pairs = (
        (key_hbm, key_ref),
        (query_hbm, query_ref),
        (decay_log_hbm, decay_log_ref),
        (step_bias_hbm, step_bias_ref),
        (decay_in_hbm, decay_in_ref),
        (beta_in_hbm, beta_in_ref),
        (norm_gain_hbm, norm_gain_ref),
        (value_hbm, value_ref),
        (gate_hbm, gate_ref),
        (ids_hbm, ids_ref),
        (hidden_hbm, hidden_ref),
        (post_gain_hbm, post_gain_ref),
        (router_hbm, router_ref),
    )
    small = [pltpu.make_async_copy(a, b, small_sem.at[i]) for i, (a, b) in enumerate(pairs)]
    early, late = small[:9], small[9:]
    for copy in early[:2]:
        copy.start()
    state_copy(0).start()
    for copy in early[2:]:
        copy.start()
    for h in range(1, key_heads):
        state_copy(h).start()
    for c in range(chunks):
        proj_copy(c).start()
    for copy in late:
        copy.start()
    for copy in early:
        copy.wait()

    query_all = query_ref[...].astype(f32)
    key_all = key_ref[...].astype(f32)
    value_all = value_ref[...].astype(f32)
    gate_all = gate_ref[...].astype(f32)
    decay_in = decay_in_ref[...].astype(f32)
    beta_in = beta_in_ref[...].astype(f32)
    rate = -jnp.exp(decay_log_ref[...].reshape(1, value_heads))
    bias = step_bias_ref[...].reshape(1, value_heads)
    decays, betas = [], []
    for p in range(2):
        decays.append(jnp.exp(rate * jax.nn.softplus(decay_in[:, p, :] + bias)))
        betas.append(1.0 / (1.0 + jnp.exp(-beta_in[:, p, :])))
    gain = norm_gain_ref[...].reshape(1, value_size)

    mixed = [[], []]
    for h in range(key_heads):
        lanes = slice(h * key_size, (h + 1) * key_size)
        keys, queries = [], []
        for p in range(2):
            k = key_all[:, p, lanes]
            q = query_all[:, p, lanes]
            keys.append(k * lax.rsqrt(jnp.sum(k * k, axis=-1, keepdims=True) + eps_norm))
            queries.append(
                q
                * lax.rsqrt(jnp.sum(q * q, axis=-1, keepdims=True) + eps_norm)
                * key_size ** (-0.5)
            )
        vectors = (keys[0], queries[0], keys[1], queries[1])
        for j, v in enumerate(vectors):
            high = v.astype(bf16).astype(f32)
            left_buf[h, pl.ds(2 * j, rows, stride=8), :] = high
            left_buf[h, pl.ds(2 * j + 1, rows, stride=8), :] = v - high
        key_key = jnp.sum(keys[0] * keys[1], axis=-1, keepdims=True)
        key_query00 = jnp.sum(keys[0] * queries[0], axis=-1, keepdims=True)
        key_query01 = jnp.sum(keys[0] * queries[1], axis=-1, keepdims=True)
        key_query11 = jnp.sum(keys[1] * queries[1], axis=-1, keepdims=True)

        state_copy(h).wait()
        for r in range(rows):
            left = left_buf[h, r * 8 : (r + 1) * 8, :].astype(bf16)
            right = jnp.concatenate([state_buf[h, r, i] for i in range(share)], axis=-1)
            out = jnp.dot(left, right, preferred_element_type=f32)
            for i in range(share):
                right_buf[h, i, r * 8 : (r + 1) * 8, :] = out[:, i * value_size : (i + 1) * value_size]

        for i in range(share):
            n = h * share + i
            heads = slice(n * value_size, (n + 1) * value_size)
            part = [
                right_buf[h, i, pl.ds(2 * j, rows, stride=8), :]
                + right_buf[h, i, pl.ds(2 * j + 1, rows, stride=8), :]
                for j in range(4)
            ]
            d0, d1 = decays[0][:, n : n + 1], decays[1][:, n : n + 1]
            b0, b1 = betas[0][:, n : n + 1], betas[1][:, n : n + 1]
            u0 = b0 * (value_all[:, 0, heads] - d0 * part[0])
            o0 = d0 * part[1] + key_query00 * u0
            u1 = b1 * (value_all[:, 1, heads] - d1 * (d0 * part[2] + key_key * u0))
            o1 = d1 * (d0 * part[3] + key_query01 * u0) + key_query11 * u1
            for p, o in enumerate((o0, o1)):
                g = gate_all[:, p, heads]
                mean = jnp.mean(o * o, axis=-1, keepdims=True)
                mixed[p].append(
                    o * lax.rsqrt(mean + eps_norm) * gain * (g / (1.0 + jnp.exp(-g)))
                )

    mixer_out = jnp.concatenate(
        [jnp.concatenate(mixed[p], axis=-1) for p in range(2)], axis=0
    ).astype(bf16)
    for copy in late:
        copy.wait()
    hidden = hidden_ref[...].astype(f32)
    total = jnp.concatenate([hidden[:, p, :] for p in range(2)], axis=0)
    for c in range(chunks):
        proj_copy(c).wait()
        part = slice(c * depth, (c + 1) * depth)
        total = total + jnp.dot(mixer_out[:, part], proj_buf[part, :], preferred_element_type=f32)
    middle = total.astype(bf16)
    middle_ref[...] = middle
    wide = middle.astype(f32)
    routed = (
        wide
        * lax.rsqrt(jnp.mean(wide * wide, axis=-1, keepdims=True) + eps_norm)
        * post_gain_ref[...].reshape(1, wide.shape[1])
    ).astype(bf16)
    logits = nt_dot(routed, router_ref[...])

    tokens = 2 * rows
    experts = logits.shape[1]
    ids = jnp.concatenate([ids_ref[:, p, :] for p in range(2)], axis=0)
    expert = lax.broadcasted_iota(jnp.int32, (tokens, experts), 1)
    chosen = jnp.zeros((tokens, experts), f32)
    for k in range(ids.shape[1]):
        chosen = chosen + (ids[:, k : k + 1] == expert).astype(f32)
    raised = jnp.where(chosen > 0.0, jnp.exp(logits), 0.0)
    high, low = split_two(raised / jnp.sum(raised, axis=-1, keepdims=True))
    width = routed.shape[1]
    extra = routed_ref.shape[1] - width
    lane = lax.broadcasted_iota(jnp.int32, (experts, extra), 1)
    number = lax.broadcasted_iota(jnp.int32, (experts, extra), 0)
    beside = jnp.dot(high, (lane == number).astype(bf16), preferred_element_type=f32)
    beside += jnp.dot(low, (lane == number + experts).astype(bf16), preferred_element_type=f32)
    routed_ref[:, :width] = routed
    routed_ref[:, width:] = beside.astype(bf16)


def column_kernel(*refs):
    out_ref = refs[-1]
    rows = refs[0].shape[0]
    for i, ref in enumerate(refs[:-1]):
        out_ref[i * rows : (i + 1) * rows, :] = ref[...]


def expert_sum(rows, width, weights, first, experts):
    hidden_units = weights[0][1].shape[1]
    x = rows[:, :width]
    beside = rows[:, width:].astype(f32)
    lane = lax.broadcasted_iota(jnp.int32, beside.shape, 1)
    total = None
    for (up_ref, down_ref), e in zip(weights, first):
        both = jnp.dot(x, up_ref[0], preferred_element_type=f32)
        g = both[:, :hidden_units]
        activated = (g / (1.0 + jnp.exp(-g)) * both[:, hidden_units:]).astype(bf16)
        result = jnp.dot(activated, down_ref[0], preferred_element_type=f32).astype(bf16)
        share = jnp.sum(jnp.where(lane == e, beside, 0.0), axis=-1, keepdims=True)
        low_lane = lane == e + experts
        share = share + jnp.sum(jnp.where(low_lane, beside, 0.0), axis=-1, keepdims=True)
        part = share * result.astype(f32)
        total = part if total is None else total + part
    return total


def expert_kernel(experts, count, *refs):
    blocks = refs[:count]
    up_own, down_own, up_other, down_other = refs[count : count + 4]
    outs = refs[count + 4 :]
    width = outs[0].shape[1]
    me = lax.axis_index("dp")
    weights = ((up_own, down_own), (up_other, down_other))
    rows = blocks[0].shape[0]
    x = blocks[0][...] if count == 1 else jnp.concatenate([b[...] for b in blocks], axis=0)
    total = expert_sum(x, width, weights, (me, me ^ 1), experts)
    for i, out in enumerate(outs):
        out[...] = total[i * rows : (i + 1) * rows].astype(out.dtype)


def column_sum_kernel(tokens, *refs):
    own_ref = refs[0]
    count = (own_ref.shape[0] // tokens)
    outs = refs[-count:]
    total = own_ref[...]
    for ref in refs[1:-count]:
        total = total + ref[...].astype(f32)
    for i, out in enumerate(outs):
        out[...] = total[i * tokens : (i + 1) * tokens].astype(out.dtype)


def final_kernel(*refs):
    out_ref = refs[-1]
    rows = out_ref.shape[0]
    total = refs[0][...].astype(f32) + refs[1][...]
    for ref in refs[2:-1]:
        total = total + ref[...].astype(f32)
    total = total.astype(bf16)
    for p in range(2):
        out_ref[:, p, :] = total[p * rows : (p + 1) * rows]


def chip_masks(device_count):
    bits = device_count.bit_length() - 2
    low = bits // 2
    near = [m << 1 for m in range(1, 1 << low)]
    far = [m << (1 + low) for m in range(1, 1 << (bits - low))]
    return near, far


def hop(x, mask):
    count = lax.axis_size("dp")
    return lax.ppermute(x, "dp", [(i, i ^ mask) for i in range(count)])


def vmem(count):
    return [pl.BlockSpec(memory_space=pltpu.VMEM)] * count


def shards(
    hidden_in,
    query_in,
    key_in,
    value_in,
    gate_in,
    decay_in,
    beta_in,
    decay_log,
    step_bias,
    norm_gain,
    state_in,
    out_proj,
    post_gain,
    router_weight,
    expert_gate_up,
    expert_down,
    expert_ids,
):
    device_count = lax.axis_size("dp")
    expert_total = expert_gate_up.shape[0] * device_count
    row_count, _, model_width = hidden_in.shape
    value_heads, key_size, value_size = state_in.shape[1:]
    key_heads = query_in.shape[2] // key_size
    share = value_heads // key_heads
    token_count = row_count * 2
    sent_width = model_width + (2 * expert_total + 127) // 128 * 128
    near, far = chip_masks(device_count)
    chunks = 4
    params = pltpu.CompilerParams(vmem_limit_bytes=48 * 1024 * 1024)
    operands = (
        hidden_in,
        query_in,
        key_in,
        value_in,
        gate_in,
        decay_in,
        beta_in,
        decay_log,
        step_bias,
        norm_gain,
        post_gain,
        router_weight.T,
        expert_ids,
        state_in,
        out_proj,
    )
    operands = [pltpu.with_memory_space_constraint(x, pltpu.HBM) for x in operands]
    up_other, down_other = hop(expert_gate_up, 1), hop(expert_down, 1)
    routed, middle = pl.pallas_call(
        mixer_kernel,
        out_shape=(
            jax.ShapeDtypeStruct((token_count, sent_width), bf16),
            jax.ShapeDtypeStruct((token_count, model_width), bf16),
        ),
        in_specs=[pl.BlockSpec(memory_space=pltpu.HBM)] * len(operands),
        out_specs=tuple(vmem(2)),
        scratch_shapes=[pltpu.VMEM(x.shape, x.dtype) for x in operands[:13]]
        + [
            pltpu.VMEM((key_heads, row_count, share, key_size, value_size), bf16),
            pltpu.VMEM(out_proj.shape, bf16),
            pltpu.VMEM((key_heads, 8 * row_count, key_size), f32),
            pltpu.VMEM((key_heads, share, 8 * row_count, value_size), f32),
            pltpu.SemaphoreType.DMA((13,)),
            pltpu.SemaphoreType.DMA((key_heads,)),
            pltpu.SemaphoreType.DMA((chunks,)),
        ],
        compiler_params=params,
        name="mixer",
    )(*operands)

    def local(body, name, outs, *args):
        return pl.pallas_call(
            body,
            out_shape=tuple(jax.ShapeDtypeStruct(*o) for o in outs),
            in_specs=vmem(len(args)),
            out_specs=tuple(vmem(len(outs))),
            compiler_params=params,
            name=name,
        )(*args)

    weights = (expert_gate_up, expert_down, up_other, down_other)
    column_rows = token_count * (len(far) + 1)
    pieces = [hop(routed, m) for m in far]
    (column,) = local(
        column_kernel, "column", [((column_rows, sent_width), bf16)], routed, *pieces
    )
    columns = [hop(column, m) for m in near]
    (own,) = local(
        functools.partial(expert_kernel, expert_total, 1),
        "own_experts",
        [((column_rows, model_width), f32)],
        column,
        *weights,
    )
    results = local(
        functools.partial(expert_kernel, expert_total, len(near)),
        "experts",
        [((column_rows, model_width), bf16)] * len(near),
        *columns,
        *weights,
    )
    back = [hop(r, m) for r, m in zip(results, near)]
    mine, *others = local(
        functools.partial(column_sum_kernel, token_count),
        "column_sum",
        [((token_count, model_width), f32)] + [((token_count, model_width), bf16)] * len(far),
        own,
        *back,
    )
    home = [hop(r, m) for r, m in zip(others, far)]
    (out,) = local(final_kernel, "final", [(hidden_in.shape, bf16)], middle, mine, *home)
    return out


def solution(mesh):
    rows = P(("groups", "dp"))
    placed = (
        (rows,) * 7 + (P(),) * 3 + (rows,) + (P(),) * 3 + (P("dp"),) * 2 + (rows,)
    )
    return jax.shard_map(
        shards,
        mesh=mesh,
        in_specs=placed,
        out_specs=rows,
        check_vma=False,
    )
```

```python
import functools

import jax
import jax.numpy as jnp
from jax import lax
from jax.experimental import pallas as pl
from jax.experimental.pallas import tpu as pltpu
from jax.sharding import PartitionSpec as P

eps_norm = 1e-06
f32 = jnp.float32
bf16 = jnp.bfloat16


def split_two(x):
    high = x.astype(bf16)
    low = (x - high.astype(f32)).astype(bf16)
    return high, low


def nt_dot(a, b):
    return lax.dot_general(a, b, (((1,), (1,)), ((), ())), preferred_element_type=f32)


def mixer_kernel(
    hidden_hbm,
    query_hbm,
    key_hbm,
    value_hbm,
    gate_hbm,
    decay_in_hbm,
    beta_in_hbm,
    decay_log_hbm,
    step_bias_hbm,
    norm_gain_hbm,
    post_gain_hbm,
    router_hbm,
    ids_hbm,
    state_hbm,
    proj_hbm,
    routed_ref,
    middle_ref,
    hidden_ref,
    query_ref,
    key_ref,
    value_ref,
    gate_ref,
    decay_in_ref,
    beta_in_ref,
    decay_log_ref,
    step_bias_ref,
    norm_gain_ref,
    post_gain_ref,
    router_ref,
    ids_ref,
    state_buf,
    proj_buf,
    left_buf,
    right_buf,
    small_sem,
    state_sem,
    proj_sem,
):
    rows = query_ref.shape[0]
    value_heads, key_size, value_size = state_hbm.shape[1:]
    key_heads = query_ref.shape[2] // key_size
    share = value_heads // key_heads
    span = share * value_size
    chunks = proj_sem.shape[0]
    depth = proj_hbm.shape[0] // chunks

    def state_copy(h):
        return pltpu.make_async_copy(
            state_hbm.at[:, pl.ds(h * share, share)], state_buf.at[h], state_sem.at[h]
        )

    def proj_copy(c):
        part = pl.ds(c * depth, depth)
        return pltpu.make_async_copy(proj_hbm.at[part], proj_buf.at[part], proj_sem.at[c])

    pairs = (
        (key_hbm, key_ref),
        (query_hbm, query_ref),
        (decay_log_hbm, decay_log_ref),
        (step_bias_hbm, step_bias_ref),
        (decay_in_hbm, decay_in_ref),
        (beta_in_hbm, beta_in_ref),
        (norm_gain_hbm, norm_gain_ref),
        (value_hbm, value_ref),
        (gate_hbm, gate_ref),
        (ids_hbm, ids_ref),
        (hidden_hbm, hidden_ref),
        (post_gain_hbm, post_gain_ref),
        (router_hbm, router_ref),
    )
    small = [pltpu.make_async_copy(a, b, small_sem.at[i]) for i, (a, b) in enumerate(pairs)]
    early, late = small[:9], small[9:]
    for copy in early[:2]:
        copy.start()
    state_copy(0).start()
    for copy in early[2:]:
        copy.start()
    for h in range(1, key_heads):
        state_copy(h).start()
    for c in range(chunks):
        proj_copy(c).start()
    for copy in late:
        copy.start()
    for copy in early:
        copy.wait()

    query_all = query_ref[...].astype(f32)
    key_all = key_ref[...].astype(f32)
    value_all = value_ref[...].astype(f32)
    gate_all = gate_ref[...].astype(f32)
    decay_in = decay_in_ref[...].astype(f32)
    beta_in = beta_in_ref[...].astype(f32)
    rate = -jnp.exp(decay_log_ref[...].reshape(1, value_heads))
    bias = step_bias_ref[...].reshape(1, value_heads)
    decays, betas = [], []
    for p in range(2):
        decays.append(jnp.exp(rate * jax.nn.softplus(decay_in[:, p, :] + bias)))
        betas.append(1.0 / (1.0 + jnp.exp(-beta_in[:, p, :])))
    gain = norm_gain_ref[...].reshape(1, value_size)

    mixed = [[], []]
    for h in range(key_heads):
        lanes = slice(h * key_size, (h + 1) * key_size)
        keys, queries = [], []
        for p in range(2):
            k = key_all[:, p, lanes]
            q = query_all[:, p, lanes]
            keys.append(k * lax.rsqrt(jnp.sum(k * k, axis=-1, keepdims=True) + eps_norm))
            queries.append(
                q
                * lax.rsqrt(jnp.sum(q * q, axis=-1, keepdims=True) + eps_norm)
                * key_size ** (-0.5)
            )
        vectors = (keys[0], queries[0], keys[1], queries[1])
        for j, v in enumerate(vectors):
            high = v.astype(bf16).astype(f32)
            left_buf[h, pl.ds(2 * j, rows, stride=8), :] = high
            left_buf[h, pl.ds(2 * j + 1, rows, stride=8), :] = v - high
        key_key = jnp.sum(keys[0] * keys[1], axis=-1, keepdims=True)
        key_query00 = jnp.sum(keys[0] * queries[0], axis=-1, keepdims=True)
        key_query01 = jnp.sum(keys[0] * queries[1], axis=-1, keepdims=True)
        key_query11 = jnp.sum(keys[1] * queries[1], axis=-1, keepdims=True)

        state_copy(h).wait()
        for r in range(rows):
            left = left_buf[h, r * 8 : (r + 1) * 8, :].astype(bf16)
            right = jnp.concatenate([state_buf[h, r, i] for i in range(share)], axis=-1)
            out = jnp.dot(left, right, preferred_element_type=f32)
            for i in range(share):
                right_buf[h, i, r * 8 : (r + 1) * 8, :] = out[:, i * value_size : (i + 1) * value_size]

        for i in range(share):
            n = h * share + i
            heads = slice(n * value_size, (n + 1) * value_size)
            part = [
                right_buf[h, i, pl.ds(2 * j, rows, stride=8), :]
                + right_buf[h, i, pl.ds(2 * j + 1, rows, stride=8), :]
                for j in range(4)
            ]
            d0, d1 = decays[0][:, n : n + 1], decays[1][:, n : n + 1]
            b0, b1 = betas[0][:, n : n + 1], betas[1][:, n : n + 1]
            u0 = b0 * (value_all[:, 0, heads] - d0 * part[0])
            o0 = d0 * part[1] + key_query00 * u0
            u1 = b1 * (value_all[:, 1, heads] - d1 * (d0 * part[2] + key_key * u0))
            o1 = d1 * (d0 * part[3] + key_query01 * u0) + key_query11 * u1
            for p, o in enumerate((o0, o1)):
                g = gate_all[:, p, heads]
                mean = jnp.mean(o * o, axis=-1, keepdims=True)
                mixed[p].append(
                    o * lax.rsqrt(mean + eps_norm) * gain * (g / (1.0 + jnp.exp(-g)))
                )

    mixer_out = jnp.concatenate(
        [jnp.concatenate(mixed[p], axis=-1) for p in range(2)], axis=0
    ).astype(bf16)
    for copy in late:
        copy.wait()
    hidden = hidden_ref[...].astype(f32)
    total = jnp.concatenate([hidden[:, p, :] for p in range(2)], axis=0)
    for c in range(chunks):
        proj_copy(c).wait()
        part = slice(c * depth, (c + 1) * depth)
        total = total + jnp.dot(mixer_out[:, part], proj_buf[part, :], preferred_element_type=f32)
    middle = total.astype(bf16)
    middle_ref[...] = middle
    wide = middle.astype(f32)
    routed = (
        wide
        * lax.rsqrt(jnp.mean(wide * wide, axis=-1, keepdims=True) + eps_norm)
        * post_gain_ref[...].reshape(1, wide.shape[1])
    ).astype(bf16)
    logits = nt_dot(routed, router_ref[...])

    tokens = 2 * rows
    experts = logits.shape[1]
    ids = jnp.concatenate([ids_ref[:, p, :] for p in range(2)], axis=0)
    expert = lax.broadcasted_iota(jnp.int32, (tokens, experts), 1)
    chosen = jnp.zeros((tokens, experts), f32)
    for k in range(ids.shape[1]):
        chosen = chosen + (ids[:, k : k + 1] == expert).astype(f32)
    raised = jnp.where(chosen > 0.0, jnp.exp(logits), 0.0)
    high, low = split_two(raised / jnp.sum(raised, axis=-1, keepdims=True))
    width = routed.shape[1]
    extra = routed_ref.shape[1] - width
    lane = lax.broadcasted_iota(jnp.int32, (experts, extra), 1)
    number = lax.broadcasted_iota(jnp.int32, (experts, extra), 0)
    beside = jnp.dot(high, (lane == number).astype(bf16), preferred_element_type=f32)
    beside += jnp.dot(low, (lane == number + experts).astype(bf16), preferred_element_type=f32)
    routed_ref[:, :width] = routed
    routed_ref[:, width:] = beside.astype(bf16)


def column_kernel(*refs):
    out_ref = refs[-1]
    rows = refs[0].shape[0]
    for i, ref in enumerate(refs[:-1]):
        out_ref[i * rows : (i + 1) * rows, :] = ref[...]


def expert_sum(rows, width, weights, first, experts):
    hidden_units = weights[0][1].shape[1]
    x = rows[:, :width]
    beside = rows[:, width:].astype(f32)
    lane = lax.broadcasted_iota(jnp.int32, beside.shape, 1)
    total = None
    for (up_ref, down_ref), e in zip(weights, first):
        both = jnp.dot(x, up_ref[0], preferred_element_type=f32)
        g = both[:, :hidden_units]
        activated = (g / (1.0 + jnp.exp(-g)) * both[:, hidden_units:]).astype(bf16)
        result = jnp.dot(activated, down_ref[0], preferred_element_type=f32).astype(bf16)
        share = jnp.sum(jnp.where(lane == e, beside, 0.0), axis=-1, keepdims=True)
        low_lane = lane == e + experts
        share = share + jnp.sum(jnp.where(low_lane, beside, 0.0), axis=-1, keepdims=True)
        part = share * result.astype(f32)
        total = part if total is None else total + part
    return total


def expert_kernel(experts, count, *refs):
    blocks = refs[:count]
    up_own, down_own, up_other, down_other = refs[count : count + 4]
    outs = refs[count + 4 :]
    width = outs[0].shape[1]
    me = lax.axis_index("dp")
    weights = ((up_own, down_own), (up_other, down_other))
    rows = blocks[0].shape[0]
    x = blocks[0][...] if count == 1 else jnp.concatenate([b[...] for b in blocks], axis=0)
    total = expert_sum(x, width, weights, (me, me ^ 1), experts)
    for i, out in enumerate(outs):
        out[...] = total[i * rows : (i + 1) * rows].astype(out.dtype)


def column_sum_kernel(tokens, *refs):
    own_ref = refs[0]
    count = (own_ref.shape[0] // tokens)
    outs = refs[-count:]
    total = own_ref[...]
    for ref in refs[1:-count]:
        total = total + ref[...].astype(f32)
    for i, out in enumerate(outs):
        out[...] = total[i * tokens : (i + 1) * tokens].astype(out.dtype)


def final_kernel(*refs):
    out_ref = refs[-1]
    rows = out_ref.shape[0]
    total = refs[0][...].astype(f32) + refs[1][...]
    for ref in refs[2:-1]:
        total = total + ref[...].astype(f32)
    total = total.astype(bf16)
    for p in range(2):
        out_ref[:, p, :] = total[p * rows : (p + 1) * rows]


def chip_masks(device_count):
    bits = device_count.bit_length() - 2
    low = bits // 2
    near = [m << 1 for m in range(1, 1 << low)]
    far = [m << (1 + low) for m in range(1, 1 << (bits - low))]
    if len(near) != len(far):
        return list(zip(far, far)), list(zip(near, near))
    return list(zip(far, near)), list(zip(near, far))


def hop(x, masks):
    count = lax.axis_size("dp")
    return lax.ppermute(x, "dp", [(i, i ^ masks[i % 2]) for i in range(count)])


def vmem(count):
    return [pl.BlockSpec(memory_space=pltpu.VMEM)] * count


def shards(
    hidden_in,
    query_in,
    key_in,
    value_in,
    gate_in,
    decay_in,
    beta_in,
    decay_log,
    step_bias,
    norm_gain,
    state_in,
    out_proj,
    post_gain,
    router_weight,
    expert_gate_up,
    expert_down,
    expert_ids,
):
    device_count = lax.axis_size("dp")
    expert_total = expert_gate_up.shape[0] * device_count
    row_count, _, model_width = hidden_in.shape
    value_heads, key_size, value_size = state_in.shape[1:]
    key_heads = query_in.shape[2] // key_size
    share = value_heads // key_heads
    token_count = row_count * 2
    sent_width = model_width + (2 * expert_total + 127) // 128 * 128
    first, second = chip_masks(device_count)
    chunks = 4
    params = pltpu.CompilerParams(vmem_limit_bytes=48 * 1024 * 1024)
    operands = (
        hidden_in,
        query_in,
        key_in,
        value_in,
        gate_in,
        decay_in,
        beta_in,
        decay_log,
        step_bias,
        norm_gain,
        post_gain,
        router_weight.T,
        expert_ids,
        state_in,
        out_proj,
    )
    operands = [pltpu.with_memory_space_constraint(x, pltpu.HBM) for x in operands]
    up_other, down_other = hop(expert_gate_up, (1, 1)), hop(expert_down, (1, 1))
    routed, middle = pl.pallas_call(
        mixer_kernel,
        out_shape=(
            jax.ShapeDtypeStruct((token_count, sent_width), bf16),
            jax.ShapeDtypeStruct((token_count, model_width), bf16),
        ),
        in_specs=[pl.BlockSpec(memory_space=pltpu.HBM)] * len(operands),
        out_specs=tuple(vmem(2)),
        scratch_shapes=[pltpu.VMEM(x.shape, x.dtype) for x in operands[:13]]
        + [
            pltpu.VMEM((key_heads, row_count, share, key_size, value_size), bf16),
            pltpu.VMEM(out_proj.shape, bf16),
            pltpu.VMEM((key_heads, 8 * row_count, key_size), f32),
            pltpu.VMEM((key_heads, share, 8 * row_count, value_size), f32),
            pltpu.SemaphoreType.DMA((13,)),
            pltpu.SemaphoreType.DMA((key_heads,)),
            pltpu.SemaphoreType.DMA((chunks,)),
        ],
        compiler_params=params,
        name="mixer",
    )(*operands)

    def local(body, name, outs, *args):
        return pl.pallas_call(
            body,
            out_shape=tuple(jax.ShapeDtypeStruct(*o) for o in outs),
            in_specs=vmem(len(args)),
            out_specs=tuple(vmem(len(outs))),
            compiler_params=params,
            name=name,
        )(*args)

    weights = (expert_gate_up, expert_down, up_other, down_other)
    column_rows = token_count * (len(first) + 1)
    pieces = [hop(routed, m) for m in first]
    (column,) = local(
        column_kernel, "column", [((column_rows, sent_width), bf16)], routed, *pieces
    )
    columns = [hop(column, m) for m in second]
    (own,) = local(
        functools.partial(expert_kernel, expert_total, 1),
        "own_experts",
        [((column_rows, model_width), f32)],
        column,
        *weights,
    )
    results = local(
        functools.partial(expert_kernel, expert_total, len(second)),
        "experts",
        [((column_rows, model_width), bf16)] * len(second),
        *columns,
        *weights,
    )
    back = [hop(r, m) for r, m in zip(results[::-1], second[::-1])]
    mine, *others = local(
        functools.partial(column_sum_kernel, token_count),
        "column_sum",
        [((token_count, model_width), f32)] + [((token_count, model_width), bf16)] * len(first),
        own,
        *back,
    )
    home = [hop(r, m) for r, m in zip(others[::-1], first[::-1])]
    (out,) = local(final_kernel, "final", [(hidden_in.shape, bf16)], middle, mine, *home)
    return out


def solution(mesh):
    rows = P(("groups", "dp"))
    placed = (
        (rows,) * 7 + (P(),) * 3 + (rows,) + (P(),) * 3 + (P("dp"),) * 2 + (rows,)
    )
    return jax.shard_map(
        shards,
        mesh=mesh,
        in_specs=placed,
        out_specs=rows,
        check_vma=False,
    )
```

```python
import functools

import jax
import jax.numpy as jnp
from jax import lax
from jax.experimental import pallas as pl
from jax.experimental.pallas import tpu as pltpu
from jax.sharding import PartitionSpec as P

eps_norm = 1e-06
f32 = jnp.float32
bf16 = jnp.bfloat16


def split_two(x):
    high = x.astype(bf16)
    low = (x - high.astype(f32)).astype(bf16)
    return high, low


def nt_dot(a, b):
    return lax.dot_general(a, b, (((1,), (1,)), ((), ())), preferred_element_type=f32)


def mixer_kernel(
    hidden_hbm,
    query_hbm,
    key_hbm,
    value_hbm,
    gate_hbm,
    decay_in_hbm,
    beta_in_hbm,
    decay_log_hbm,
    step_bias_hbm,
    norm_gain_hbm,
    post_gain_hbm,
    router_hbm,
    ids_hbm,
    state_hbm,
    proj_hbm,
    routed_ref,
    middle_ref,
    hidden_ref,
    query_ref,
    key_ref,
    value_ref,
    gate_ref,
    decay_in_ref,
    beta_in_ref,
    decay_log_ref,
    step_bias_ref,
    norm_gain_ref,
    post_gain_ref,
    router_ref,
    ids_ref,
    state_buf,
    proj_buf,
    left_buf,
    right_buf,
    small_sem,
    state_sem,
    proj_sem,
):
    rows = query_ref.shape[0]
    value_heads, key_size, value_size = state_hbm.shape[1:]
    key_heads = query_ref.shape[2] // key_size
    share = value_heads // key_heads
    span = share * value_size
    chunks = proj_sem.shape[0]
    depth = proj_hbm.shape[0] // chunks

    groups = state_sem.shape[0]
    group = key_heads // groups

    def state_copy(c):
        part = pl.ds(c * group * share, group * share)
        return pltpu.make_async_copy(
            state_hbm.at[:, part], state_buf.at[:, part], state_sem.at[c]
        )

    def proj_copy(c):
        part = pl.ds(c * depth, depth)
        return pltpu.make_async_copy(proj_hbm.at[part], proj_buf.at[part], proj_sem.at[c])

    pairs = (
        (key_hbm, key_ref),
        (query_hbm, query_ref),
        (decay_log_hbm, decay_log_ref),
        (step_bias_hbm, step_bias_ref),
        (decay_in_hbm, decay_in_ref),
        (beta_in_hbm, beta_in_ref),
        (norm_gain_hbm, norm_gain_ref),
        (value_hbm, value_ref),
        (gate_hbm, gate_ref),
        (ids_hbm, ids_ref),
        (hidden_hbm, hidden_ref),
        (post_gain_hbm, post_gain_ref),
        (router_hbm, router_ref),
    )
    small = [pltpu.make_async_copy(a, b, small_sem.at[i]) for i, (a, b) in enumerate(pairs)]
    early, late = small[:9], small[9:]
    for copy in early[:2]:
        copy.start()
    state_copy(0).start()
    for copy in early[2:]:
        copy.start()
    for c in range(1, groups):
        state_copy(c).start()
    for c in range(chunks):
        proj_copy(c).start()
    for copy in late:
        copy.start()
    for copy in early:
        copy.wait()

    query_all = query_ref[...].astype(f32)
    key_all = key_ref[...].astype(f32)
    value_all = value_ref[...].astype(f32)
    gate_all = gate_ref[...].astype(f32)
    decay_in = decay_in_ref[...].astype(f32)
    beta_in = beta_in_ref[...].astype(f32)
    rate = -jnp.exp(decay_log_ref[...].reshape(1, value_heads))
    bias = step_bias_ref[...].reshape(1, value_heads)
    decays, betas = [], []
    for p in range(2):
        decays.append(jnp.exp(rate * jax.nn.softplus(decay_in[:, p, :] + bias)))
        betas.append(1.0 / (1.0 + jnp.exp(-beta_in[:, p, :])))
    gain = norm_gain_ref[...].reshape(1, value_size)

    mixed = [[], []]
    for h in range(key_heads):
        lanes = slice(h * key_size, (h + 1) * key_size)
        keys, queries = [], []
        for p in range(2):
            k = key_all[:, p, lanes]
            q = query_all[:, p, lanes]
            keys.append(k * lax.rsqrt(jnp.sum(k * k, axis=-1, keepdims=True) + eps_norm))
            queries.append(
                q
                * lax.rsqrt(jnp.sum(q * q, axis=-1, keepdims=True) + eps_norm)
                * key_size ** (-0.5)
            )
        vectors = (keys[0], queries[0], keys[1], queries[1])
        for j, v in enumerate(vectors):
            high = v.astype(bf16).astype(f32)
            left_buf[h, pl.ds(2 * j, rows, stride=8), :] = high
            left_buf[h, pl.ds(2 * j + 1, rows, stride=8), :] = v - high
        key_key = jnp.sum(keys[0] * keys[1], axis=-1, keepdims=True)
        key_query00 = jnp.sum(keys[0] * queries[0], axis=-1, keepdims=True)
        key_query01 = jnp.sum(keys[0] * queries[1], axis=-1, keepdims=True)
        key_query11 = jnp.sum(keys[1] * queries[1], axis=-1, keepdims=True)

        if h % group == 0:
            state_copy(h // group).wait()
        for r in range(rows):
            left = left_buf[h, r * 8 : (r + 1) * 8, :].astype(bf16)
            right = jnp.concatenate([state_buf[r, h * share + i] for i in range(share)], axis=-1)
            out = jnp.dot(left, right, preferred_element_type=f32)
            for i in range(share):
                right_buf[h, i, r * 8 : (r + 1) * 8, :] = out[:, i * value_size : (i + 1) * value_size]

        for i in range(share):
            n = h * share + i
            heads = slice(n * value_size, (n + 1) * value_size)
            part = [
                right_buf[h, i, pl.ds(2 * j, rows, stride=8), :]
                + right_buf[h, i, pl.ds(2 * j + 1, rows, stride=8), :]
                for j in range(4)
            ]
            d0, d1 = decays[0][:, n : n + 1], decays[1][:, n : n + 1]
            b0, b1 = betas[0][:, n : n + 1], betas[1][:, n : n + 1]
            u0 = b0 * (value_all[:, 0, heads] - d0 * part[0])
            o0 = d0 * part[1] + key_query00 * u0
            u1 = b1 * (value_all[:, 1, heads] - d1 * (d0 * part[2] + key_key * u0))
            o1 = d1 * (d0 * part[3] + key_query01 * u0) + key_query11 * u1
            for p, o in enumerate((o0, o1)):
                g = gate_all[:, p, heads]
                mean = jnp.mean(o * o, axis=-1, keepdims=True)
                mixed[p].append(
                    o * lax.rsqrt(mean + eps_norm) * gain * (g / (1.0 + jnp.exp(-g)))
                )

    mixer_out = jnp.concatenate(
        [jnp.concatenate(mixed[p], axis=-1) for p in range(2)], axis=0
    ).astype(bf16)
    for copy in late:
        copy.wait()
    hidden = hidden_ref[...].astype(f32)
    total = jnp.concatenate([hidden[:, p, :] for p in range(2)], axis=0)
    for c in range(chunks):
        proj_copy(c).wait()
        part = slice(c * depth, (c + 1) * depth)
        total = total + jnp.dot(mixer_out[:, part], proj_buf[part, :], preferred_element_type=f32)
    middle = total.astype(bf16)
    middle_ref[...] = middle
    wide = middle.astype(f32)
    routed = (
        wide
        * lax.rsqrt(jnp.mean(wide * wide, axis=-1, keepdims=True) + eps_norm)
        * post_gain_ref[...].reshape(1, wide.shape[1])
    ).astype(bf16)
    logits = nt_dot(routed, router_ref[...])

    tokens = 2 * rows
    experts = logits.shape[1]
    ids = jnp.concatenate([ids_ref[:, p, :] for p in range(2)], axis=0)
    expert = lax.broadcasted_iota(jnp.int32, (tokens, experts), 1)
    chosen = jnp.zeros((tokens, experts), f32)
    for k in range(ids.shape[1]):
        chosen = chosen + (ids[:, k : k + 1] == expert).astype(f32)
    raised = jnp.where(chosen > 0.0, jnp.exp(logits), 0.0)
    high, low = split_two(raised / jnp.sum(raised, axis=-1, keepdims=True))
    width = routed.shape[1]
    extra = routed_ref.shape[1] - width
    lane = lax.broadcasted_iota(jnp.int32, (experts, extra), 1)
    number = lax.broadcasted_iota(jnp.int32, (experts, extra), 0)
    beside = jnp.dot(high, (lane == number).astype(bf16), preferred_element_type=f32)
    beside += jnp.dot(low, (lane == number + experts).astype(bf16), preferred_element_type=f32)
    routed_ref[:, :width] = routed
    routed_ref[:, width:] = beside.astype(bf16)


def column_kernel(*refs):
    out_ref = refs[-1]
    rows = refs[0].shape[0]
    for i, ref in enumerate(refs[:-1]):
        out_ref[i * rows : (i + 1) * rows, :] = ref[...]


def expert_sum(rows, width, weights, first, experts):
    hidden_units = weights[0][1].shape[1]
    x = rows[:, :width]
    beside = rows[:, width:].astype(f32)
    lane = lax.broadcasted_iota(jnp.int32, beside.shape, 1)
    total = None
    for (up_ref, down_ref), e in zip(weights, first):
        both = jnp.dot(x, up_ref[0], preferred_element_type=f32)
        g = both[:, :hidden_units]
        activated = (g / (1.0 + jnp.exp(-g)) * both[:, hidden_units:]).astype(bf16)
        result = jnp.dot(activated, down_ref[0], preferred_element_type=f32).astype(bf16)
        share = jnp.sum(jnp.where(lane == e, beside, 0.0), axis=-1, keepdims=True)
        low_lane = lane == e + experts
        share = share + jnp.sum(jnp.where(low_lane, beside, 0.0), axis=-1, keepdims=True)
        part = share * result.astype(f32)
        total = part if total is None else total + part
    return total


def expert_kernel(experts, count, *refs):
    blocks = refs[:count]
    up_own, down_own, up_other, down_other = refs[count : count + 4]
    outs = refs[count + 4 :]
    width = outs[0].shape[1]
    me = lax.axis_index("dp")
    weights = ((up_own, down_own), (up_other, down_other))
    rows = blocks[0].shape[0]
    x = blocks[0][...] if count == 1 else jnp.concatenate([b[...] for b in blocks], axis=0)
    total = expert_sum(x, width, weights, (me, me ^ 1), experts)
    for i, out in enumerate(outs):
        out[...] = total[i * rows : (i + 1) * rows].astype(out.dtype)


def column_sum_kernel(tokens, *refs):
    own_ref = refs[0]
    count = (own_ref.shape[0] // tokens)
    outs = refs[-count:]
    total = own_ref[...]
    for ref in refs[1:-count]:
        total = total + ref[...].astype(f32)
    for i, out in enumerate(outs):
        out[...] = total[i * tokens : (i + 1) * tokens].astype(out.dtype)


def final_kernel(*refs):
    out_ref = refs[-1]
    rows = out_ref.shape[0]
    total = refs[0][...].astype(f32) + refs[1][...]
    for ref in refs[2:-1]:
        total = total + ref[...].astype(f32)
    total = total.astype(bf16)
    for p in range(2):
        out_ref[:, p, :] = total[p * rows : (p + 1) * rows]


def chip_masks(device_count):
    bits = device_count.bit_length() - 2
    low = bits // 2
    near = [m << 1 for m in range(1, 1 << low)]
    far = [m << (1 + low) for m in range(1, 1 << (bits - low))]
    if len(near) != len(far):
        return list(zip(far, far)), list(zip(near, near))
    return list(zip(far, near)), list(zip(near, far))


def hop(x, masks):
    count = lax.axis_size("dp")
    return lax.ppermute(x, "dp", [(i, i ^ masks[i % 2]) for i in range(count)])


def vmem(count):
    return [pl.BlockSpec(memory_space=pltpu.VMEM)] * count


def shards(
    hidden_in,
    query_in,
    key_in,
    value_in,
    gate_in,
    decay_in,
    beta_in,
    decay_log,
    step_bias,
    norm_gain,
    state_in,
    out_proj,
    post_gain,
    router_weight,
    expert_gate_up,
    expert_down,
    expert_ids,
):
    device_count = lax.axis_size("dp")
    expert_total = expert_gate_up.shape[0] * device_count
    row_count, _, model_width = hidden_in.shape
    value_heads, key_size, value_size = state_in.shape[1:]
    key_heads = query_in.shape[2] // key_size
    share = value_heads // key_heads
    token_count = row_count * 2
    sent_width = model_width + (2 * expert_total + 127) // 128 * 128
    first, second = chip_masks(device_count)
    chunks = 2
    params = pltpu.CompilerParams(vmem_limit_bytes=48 * 1024 * 1024)
    operands = (
        hidden_in,
        query_in,
        key_in,
        value_in,
        gate_in,
        decay_in,
        beta_in,
        decay_log,
        step_bias,
        norm_gain,
        post_gain,
        router_weight.T,
        expert_ids,
        state_in,
        out_proj,
    )
    operands = [pltpu.with_memory_space_constraint(x, pltpu.HBM) for x in operands]
    up_other, down_other = hop(expert_gate_up, (1, 1)), hop(expert_down, (1, 1))
    routed, middle = pl.pallas_call(
        mixer_kernel,
        out_shape=(
            jax.ShapeDtypeStruct((token_count, sent_width), bf16),
            jax.ShapeDtypeStruct((token_count, model_width), bf16),
        ),
        in_specs=[pl.BlockSpec(memory_space=pltpu.HBM)] * len(operands),
        out_specs=tuple(vmem(2)),
        scratch_shapes=[pltpu.VMEM(x.shape, x.dtype) for x in operands[:13]]
        + [
            pltpu.VMEM(state_in.shape, bf16),
            pltpu.VMEM(out_proj.shape, bf16),
            pltpu.VMEM((key_heads, 8 * row_count, key_size), f32),
            pltpu.VMEM((key_heads, share, 8 * row_count, value_size), f32),
            pltpu.SemaphoreType.DMA((13,)),
            pltpu.SemaphoreType.DMA((key_heads // 2,)),
            pltpu.SemaphoreType.DMA((chunks,)),
        ],
        compiler_params=params,
        name="mixer",
    )(*operands)

    def local(body, name, outs, *args):
        return pl.pallas_call(
            body,
            out_shape=tuple(jax.ShapeDtypeStruct(*o) for o in outs),
            in_specs=vmem(len(args)),
            out_specs=tuple(vmem(len(outs))),
            compiler_params=params,
            name=name,
        )(*args)

    weights = (expert_gate_up, expert_down, up_other, down_other)
    column_rows = token_count * (len(first) + 1)
    pieces = [hop(routed, m) for m in first]
    (column,) = local(
        column_kernel, "column", [((column_rows, sent_width), bf16)], routed, *pieces
    )
    columns = [hop(column, m) for m in second]
    (own,) = local(
        functools.partial(expert_kernel, expert_total, 1),
        "own_experts",
        [((column_rows, model_width), f32)],
        column,
        *weights,
    )
    results = local(
        functools.partial(expert_kernel, expert_total, len(second)),
        "experts",
        [((column_rows, model_width), bf16)] * len(second),
        *columns,
        *weights,
    )
    back = [hop(r, m) for r, m in zip(results[::-1], second[::-1])]
    mine, *others = local(
        functools.partial(column_sum_kernel, token_count),
        "column_sum",
        [((token_count, model_width), f32)] + [((token_count, model_width), bf16)] * len(first),
        own,
        *back,
    )
    home = [hop(r, m) for r, m in zip(others[::-1], first[::-1])]
    (out,) = local(final_kernel, "final", [(hidden_in.shape, bf16)], middle, mine, *home)
    return out


def solution(mesh):
    rows = P(("groups", "dp"))
    placed = (
        (rows,) * 7 + (P(),) * 3 + (rows,) + (P(),) * 3 + (P("dp"),) * 2 + (rows,)
    )
    return jax.shard_map(
        shards,
        mesh=mesh,
        in_specs=placed,
        out_specs=rows,
        check_vma=False,
    )
```

```python
import functools

import jax
import jax.numpy as jnp
from jax import lax
from jax.experimental import pallas as pl
from jax.experimental.pallas import tpu as pltpu
from jax.sharding import PartitionSpec as P

eps_norm = 1e-06
f32 = jnp.float32
bf16 = jnp.bfloat16


def nt_dot(a, b):
    return lax.dot_general(a, b, (((1,), (1,)), ((), ())), preferred_element_type=f32)


def mixer_kernel(
    hidden_hbm,
    query_hbm,
    key_hbm,
    value_hbm,
    gate_hbm,
    decay_in_hbm,
    beta_in_hbm,
    decay_log_hbm,
    step_bias_hbm,
    norm_gain_hbm,
    post_gain_hbm,
    ids_hbm,
    state_hbm,
    proj_hbm,
    routed_ref,
    middle_ref,
    hidden_ref,
    query_ref,
    key_ref,
    value_ref,
    gate_ref,
    decay_in_ref,
    beta_in_ref,
    decay_log_ref,
    step_bias_ref,
    norm_gain_ref,
    post_gain_ref,
    ids_ref,
    state_buf,
    proj_buf,
    left_buf,
    right_buf,
    small_sem,
    state_sem,
    proj_sem,
):
    rows = query_ref.shape[0]
    value_heads, key_size, value_size = state_hbm.shape[1:]
    key_heads = query_ref.shape[2] // key_size
    share = value_heads // key_heads
    span = share * value_size
    chunks = proj_sem.shape[0]
    depth = proj_hbm.shape[0] // chunks

    groups = state_sem.shape[0]
    group = key_heads // groups

    def state_copy(c):
        part = pl.ds(c * group * share, group * share)
        return pltpu.make_async_copy(
            state_hbm.at[:, part], state_buf.at[:, part], state_sem.at[c]
        )

    def proj_copy(c):
        part = pl.ds(c * depth, depth)
        return pltpu.make_async_copy(proj_hbm.at[part], proj_buf.at[part], proj_sem.at[c])

    pairs = (
        (key_hbm, key_ref),
        (query_hbm, query_ref),
        (decay_log_hbm, decay_log_ref),
        (step_bias_hbm, step_bias_ref),
        (decay_in_hbm, decay_in_ref),
        (beta_in_hbm, beta_in_ref),
        (norm_gain_hbm, norm_gain_ref),
        (value_hbm, value_ref),
        (gate_hbm, gate_ref),
        (ids_hbm, ids_ref),
        (hidden_hbm, hidden_ref),
        (post_gain_hbm, post_gain_ref),
    )
    small = [pltpu.make_async_copy(a, b, small_sem.at[i]) for i, (a, b) in enumerate(pairs)]
    early, late = small[:9], small[9:]
    for copy in early[:2]:
        copy.start()
    state_copy(0).start()
    for copy in early[2:]:
        copy.start()
    for c in range(1, groups):
        state_copy(c).start()
    for c in range(chunks):
        proj_copy(c).start()
    for copy in late:
        copy.start()
    for copy in early:
        copy.wait()

    query_all = query_ref[...].astype(f32)
    key_all = key_ref[...].astype(f32)
    value_all = value_ref[...].astype(f32)
    gate_all = gate_ref[...].astype(f32)
    decay_in = decay_in_ref[...].astype(f32)
    beta_in = beta_in_ref[...].astype(f32)
    rate = -jnp.exp(decay_log_ref[...].reshape(1, value_heads))
    bias = step_bias_ref[...].reshape(1, value_heads)
    decays, betas = [], []
    for p in range(2):
        decays.append(jnp.exp(rate * jax.nn.softplus(decay_in[:, p, :] + bias)))
        betas.append(1.0 / (1.0 + jnp.exp(-beta_in[:, p, :])))
    gain = norm_gain_ref[...].reshape(1, value_size)

    mixed = [[], []]
    for h in range(key_heads):
        lanes = slice(h * key_size, (h + 1) * key_size)
        keys, queries = [], []
        for p in range(2):
            k = key_all[:, p, lanes]
            q = query_all[:, p, lanes]
            keys.append(k * lax.rsqrt(jnp.sum(k * k, axis=-1, keepdims=True) + eps_norm))
            queries.append(
                q
                * lax.rsqrt(jnp.sum(q * q, axis=-1, keepdims=True) + eps_norm)
                * key_size ** (-0.5)
            )
        vectors = (keys[0], queries[0], keys[1], queries[1])
        for j, v in enumerate(vectors):
            high = v.astype(bf16).astype(f32)
            left_buf[h, pl.ds(2 * j, rows, stride=8), :] = high
            left_buf[h, pl.ds(2 * j + 1, rows, stride=8), :] = v - high
        key_key = jnp.sum(keys[0] * keys[1], axis=-1, keepdims=True)
        key_query00 = jnp.sum(keys[0] * queries[0], axis=-1, keepdims=True)
        key_query01 = jnp.sum(keys[0] * queries[1], axis=-1, keepdims=True)
        key_query11 = jnp.sum(keys[1] * queries[1], axis=-1, keepdims=True)

        if h % group == 0:
            state_copy(h // group).wait()
        for r in range(rows):
            left = left_buf[h, r * 8 : (r + 1) * 8, :].astype(bf16)
            right = jnp.concatenate([state_buf[r, h * share + i] for i in range(share)], axis=-1)
            out = jnp.dot(left, right, preferred_element_type=f32)
            for i in range(share):
                right_buf[h, i, r * 8 : (r + 1) * 8, :] = out[:, i * value_size : (i + 1) * value_size]

        for i in range(share):
            n = h * share + i
            heads = slice(n * value_size, (n + 1) * value_size)
            part = [
                right_buf[h, i, pl.ds(2 * j, rows, stride=8), :]
                + right_buf[h, i, pl.ds(2 * j + 1, rows, stride=8), :]
                for j in range(4)
            ]
            d0, d1 = decays[0][:, n : n + 1], decays[1][:, n : n + 1]
            b0, b1 = betas[0][:, n : n + 1], betas[1][:, n : n + 1]
            u0 = b0 * (value_all[:, 0, heads] - d0 * part[0])
            o0 = d0 * part[1] + key_query00 * u0
            u1 = b1 * (value_all[:, 1, heads] - d1 * (d0 * part[2] + key_key * u0))
            o1 = d1 * (d0 * part[3] + key_query01 * u0) + key_query11 * u1
            for p, o in enumerate((o0, o1)):
                g = gate_all[:, p, heads]
                mean = jnp.mean(o * o, axis=-1, keepdims=True)
                mixed[p].append(
                    o * lax.rsqrt(mean + eps_norm) * gain * (g / (1.0 + jnp.exp(-g)))
                )

    mixer_out = jnp.concatenate(
        [jnp.concatenate(mixed[p], axis=-1) for p in range(2)], axis=0
    ).astype(bf16)
    for copy in late:
        copy.wait()
    tokens, extra = 2 * rows, routed_ref.shape[1] - proj_hbm.shape[1]
    ids = jnp.concatenate([ids_ref[:, p, :] for p in range(2)], axis=0)
    lane = lax.broadcasted_iota(jnp.int32, (tokens, extra), 1)
    chosen = jnp.zeros((tokens, extra), f32)
    for k in range(ids.shape[1]):
        chosen = chosen + (ids[:, k : k + 1] == lane).astype(f32)
    routed_ref[:, -extra:] = chosen.astype(bf16)
    hidden = hidden_ref[...].astype(f32)
    total = jnp.concatenate([hidden[:, p, :] for p in range(2)], axis=0)
    for c in range(chunks):
        proj_copy(c).wait()
        part = slice(c * depth, (c + 1) * depth)
        total = total + jnp.dot(mixer_out[:, part], proj_buf[part, :], preferred_element_type=f32)
    middle = total.astype(bf16)
    middle_ref[...] = middle
    wide = middle.astype(f32)
    routed = (
        wide
        * lax.rsqrt(jnp.mean(wide * wide, axis=-1, keepdims=True) + eps_norm)
        * post_gain_ref[...].reshape(1, wide.shape[1])
    ).astype(bf16)
    routed_ref[:, : routed.shape[1]] = routed


def column_kernel(*refs):
    out_ref = refs[-1]
    rows = refs[0].shape[0]
    for i, ref in enumerate(refs[:-1]):
        out_ref[i * rows : (i + 1) * rows, :] = ref[...]


def expert_kernel(count, *refs):
    blocks = refs[:count]
    router, up_own, down_own, up_other, down_other = refs[count : count + 5]
    outs = refs[count + 5 :]
    rows, width = outs[0].shape
    hidden_units = down_own.shape[1]
    me = lax.axis_index("dp")
    both_parts = blocks[0][...] if count == 1 else jnp.concatenate([b[...] for b in blocks], axis=0)
    x = both_parts[:, :width]
    chosen = both_parts[:, width:].astype(f32)[:, : router.shape[0]] > 0.0
    raised = jnp.where(chosen, jnp.exp(nt_dot(x, router[...])), 0.0)
    whole = jnp.sum(raised, axis=-1, keepdims=True)
    lane = lax.broadcasted_iota(jnp.int32, raised.shape, 1)
    total = None
    for up_ref, down_ref, e in ((up_own, down_own, me), (up_other, down_other, me ^ 1)):
        both = jnp.dot(x, up_ref[0], preferred_element_type=f32)
        g = both[:, :hidden_units]
        activated = (g / (1.0 + jnp.exp(-g)) * both[:, hidden_units:]).astype(bf16)
        result = jnp.dot(activated, down_ref[0], preferred_element_type=f32).astype(bf16)
        share = jnp.sum(jnp.where(lane == e, raised, 0.0), axis=-1, keepdims=True) / whole
        part = share * result.astype(f32)
        total = part if total is None else total + part
    for i, out in enumerate(outs):
        out[...] = total[i * rows : (i + 1) * rows].astype(out.dtype)


def column_sum_kernel(tokens, *refs):
    own_ref = refs[0]
    count = (own_ref.shape[0] // tokens)
    outs = refs[-count:]
    total = own_ref[...]
    for ref in refs[1:-count]:
        total = total + ref[...].astype(f32)
    for i, out in enumerate(outs):
        out[...] = total[i * tokens : (i + 1) * tokens].astype(out.dtype)


def final_kernel(*refs):
    out_ref = refs[-1]
    rows = out_ref.shape[0]
    total = refs[0][...].astype(f32) + refs[1][...]
    for ref in refs[2:-1]:
        total = total + ref[...].astype(f32)
    total = total.astype(bf16)
    for p in range(2):
        out_ref[:, p, :] = total[p * rows : (p + 1) * rows]


def chip_masks(device_count):
    bits = device_count.bit_length() - 2
    low = bits // 2
    near = [m << 1 for m in range(1, 1 << low)]
    far = [m << (1 + low) for m in range(1, 1 << (bits - low))]
    if len(near) != len(far):
        return list(zip(far, far)), list(zip(near, near))
    return list(zip(far, near)), list(zip(near, far))


def hop(x, masks):
    count = lax.axis_size("dp")
    return lax.ppermute(x, "dp", [(i, i ^ masks[i % 2]) for i in range(count)])


def vmem(count):
    return [pl.BlockSpec(memory_space=pltpu.VMEM)] * count


def shards(
    hidden_in,
    query_in,
    key_in,
    value_in,
    gate_in,
    decay_in,
    beta_in,
    decay_log,
    step_bias,
    norm_gain,
    state_in,
    out_proj,
    post_gain,
    router_weight,
    expert_gate_up,
    expert_down,
    expert_ids,
):
    device_count = lax.axis_size("dp")
    expert_total = expert_gate_up.shape[0] * device_count
    row_count, _, model_width = hidden_in.shape
    value_heads, key_size, value_size = state_in.shape[1:]
    key_heads = query_in.shape[2] // key_size
    share = value_heads // key_heads
    token_count = row_count * 2
    sent_width = model_width + (expert_total + 127) // 128 * 128
    first, second = chip_masks(device_count)
    chunks = 2
    params = pltpu.CompilerParams(vmem_limit_bytes=48 * 1024 * 1024)
    operands = (
        hidden_in,
        query_in,
        key_in,
        value_in,
        gate_in,
        decay_in,
        beta_in,
        decay_log,
        step_bias,
        norm_gain,
        post_gain,
        expert_ids,
        state_in,
        out_proj,
    )
    operands = [pltpu.with_memory_space_constraint(x, pltpu.HBM) for x in operands]
    up_other, down_other = hop(expert_gate_up, (1, 1)), hop(expert_down, (1, 1))
    routed, middle = pl.pallas_call(
        mixer_kernel,
        out_shape=(
            jax.ShapeDtypeStruct((token_count, sent_width), bf16),
            jax.ShapeDtypeStruct((token_count, model_width), bf16),
        ),
        in_specs=[pl.BlockSpec(memory_space=pltpu.HBM)] * len(operands),
        out_specs=tuple(vmem(2)),
        scratch_shapes=[pltpu.VMEM(x.shape, x.dtype) for x in operands[:12]]
        + [
            pltpu.VMEM(state_in.shape, bf16),
            pltpu.VMEM(out_proj.shape, bf16),
            pltpu.VMEM((key_heads, 8 * row_count, key_size), f32),
            pltpu.VMEM((key_heads, share, 8 * row_count, value_size), f32),
            pltpu.SemaphoreType.DMA((12,)),
            pltpu.SemaphoreType.DMA((key_heads // 2,)),
            pltpu.SemaphoreType.DMA((chunks,)),
        ],
        compiler_params=params,
        name="mixer",
    )(*operands)

    def local(body, name, outs, *args):
        return pl.pallas_call(
            body,
            out_shape=tuple(jax.ShapeDtypeStruct(*o) for o in outs),
            in_specs=vmem(len(args)),
            out_specs=tuple(vmem(len(outs))),
            compiler_params=params,
            name=name,
        )(*args)

    weights = (router_weight.T, expert_gate_up, expert_down, up_other, down_other)
    column_rows = token_count * (len(first) + 1)
    pieces = [hop(routed, m) for m in first]
    (column,) = local(
        column_kernel, "column", [((column_rows, sent_width), bf16)], routed, *pieces
    )
    columns = [hop(column, m) for m in second]
    (own,) = local(
        functools.partial(expert_kernel, 1),
        "own_experts",
        [((column_rows, model_width), f32)],
        column,
        *weights,
    )
    results = local(
        functools.partial(expert_kernel, len(second)),
        "experts",
        [((column_rows, model_width), bf16)] * len(second),
        *columns,
        *weights,
    )
    back = [hop(r, m) for r, m in zip(results[::-1], second[::-1])]
    mine, *others = local(
        functools.partial(column_sum_kernel, token_count),
        "column_sum",
        [((token_count, model_width), f32)] + [((token_count, model_width), bf16)] * len(first),
        own,
        *back,
    )
    home = [hop(r, m) for r, m in zip(others[::-1], first[::-1])]
    (out,) = local(final_kernel, "final", [(hidden_in.shape, bf16)], middle, mine, *home)
    return out


def solution(mesh):
    rows = P(("groups", "dp"))
    placed = (
        (rows,) * 7 + (P(),) * 3 + (rows,) + (P(),) * 3 + (P("dp"),) * 2 + (rows,)
    )
    return jax.shard_map(
        shards,
        mesh=mesh,
        in_specs=placed,
        out_specs=rows,
        check_vma=False,
    )
```

```python
import functools

import jax
import jax.numpy as jnp
from jax import lax
from jax.experimental import pallas as pl
from jax.experimental.pallas import tpu as pltpu
from jax.sharding import PartitionSpec as P

eps_norm = 1e-06
f32 = jnp.float32
bf16 = jnp.bfloat16


def nt_dot(a, b):
    return lax.dot_general(a, b, (((1,), (1,)), ((), ())), preferred_element_type=f32)


def mixer_kernel(
    hidden_hbm,
    query_hbm,
    key_hbm,
    value_hbm,
    gate_hbm,
    decay_in_hbm,
    beta_in_hbm,
    decay_log_hbm,
    step_bias_hbm,
    norm_gain_hbm,
    post_gain_hbm,
    ids_hbm,
    state_hbm,
    proj_hbm,
    routed_ref,
    middle_ref,
    hidden_ref,
    query_ref,
    key_ref,
    value_ref,
    gate_ref,
    decay_in_ref,
    beta_in_ref,
    decay_log_ref,
    step_bias_ref,
    norm_gain_ref,
    post_gain_ref,
    ids_ref,
    state_buf,
    proj_buf,
    left_buf,
    right_buf,
    small_sem,
    state_sem,
    proj_sem,
):
    rows = query_ref.shape[0]
    value_heads, key_size, value_size = state_hbm.shape[1:]
    key_heads = query_ref.shape[2] // key_size
    share = value_heads // key_heads
    span = share * value_size
    chunks = proj_sem.shape[0]
    depth = proj_hbm.shape[0] // chunks

    groups = state_sem.shape[0]
    group = key_heads // groups

    def state_copy(c):
        part = pl.ds(c * group * share, group * share)
        return pltpu.make_async_copy(
            state_hbm.at[:, part], state_buf.at[:, part], state_sem.at[c]
        )

    def proj_copy(c):
        part = pl.ds(c * depth, depth)
        return pltpu.make_async_copy(proj_hbm.at[part], proj_buf.at[part], proj_sem.at[c])

    pairs = (
        (key_hbm, key_ref),
        (query_hbm, query_ref),
        (decay_log_hbm, decay_log_ref),
        (step_bias_hbm, step_bias_ref),
        (decay_in_hbm, decay_in_ref),
        (beta_in_hbm, beta_in_ref),
        (norm_gain_hbm, norm_gain_ref),
        (value_hbm, value_ref),
        (gate_hbm, gate_ref),
        (ids_hbm, ids_ref),
        (hidden_hbm, hidden_ref),
        (post_gain_hbm, post_gain_ref),
    )
    small = [pltpu.make_async_copy(a, b, small_sem.at[i]) for i, (a, b) in enumerate(pairs)]
    early, late = small[:9], small[9:]
    for copy in early[:2]:
        copy.start()
    state_copy(0).start()
    for copy in early[2:]:
        copy.start()
    for c in range(1, groups):
        state_copy(c).start()
    for c in range(chunks):
        proj_copy(c).start()
    for copy in late:
        copy.start()
    for copy in early:
        copy.wait()

    query_all = query_ref[...].astype(f32)
    key_all = key_ref[...].astype(f32)
    value_all = value_ref[...].astype(f32)
    gate_all = gate_ref[...].astype(f32)
    decay_in = decay_in_ref[...].astype(f32)
    beta_in = beta_in_ref[...].astype(f32)
    rate = -jnp.exp(decay_log_ref[...].reshape(1, value_heads))
    bias = step_bias_ref[...].reshape(1, value_heads)
    decays, betas = [], []
    for p in range(2):
        decays.append(jnp.exp(rate * jax.nn.softplus(decay_in[:, p, :] + bias)))
        betas.append(1.0 / (1.0 + jnp.exp(-beta_in[:, p, :])))
    gain = norm_gain_ref[...].reshape(1, value_size)

    mixed = [[], []]
    for h in range(key_heads):
        lanes = slice(h * key_size, (h + 1) * key_size)
        keys, queries = [], []
        for p in range(2):
            k = key_all[:, p, lanes]
            q = query_all[:, p, lanes]
            keys.append(k * lax.rsqrt(jnp.sum(k * k, axis=-1, keepdims=True) + eps_norm))
            queries.append(
                q
                * lax.rsqrt(jnp.sum(q * q, axis=-1, keepdims=True) + eps_norm)
                * key_size ** (-0.5)
            )
        vectors = (keys[0], queries[0], keys[1], queries[1])
        for j, v in enumerate(vectors):
            high = v.astype(bf16).astype(f32)
            left_buf[h, pl.ds(2 * j, rows, stride=8), :] = high
            left_buf[h, pl.ds(2 * j + 1, rows, stride=8), :] = v - high
        key_key = jnp.sum(keys[0] * keys[1], axis=-1, keepdims=True)
        key_query00 = jnp.sum(keys[0] * queries[0], axis=-1, keepdims=True)
        key_query01 = jnp.sum(keys[0] * queries[1], axis=-1, keepdims=True)
        key_query11 = jnp.sum(keys[1] * queries[1], axis=-1, keepdims=True)

        if h % group == 0:
            state_copy(h // group).wait()
        for r in range(rows):
            left = left_buf[h, r * 8 : (r + 1) * 8, :].astype(bf16)
            right = jnp.concatenate([state_buf[r, h * share + i] for i in range(share)], axis=-1)
            out = jnp.dot(left, right, preferred_element_type=f32)
            for i in range(share):
                right_buf[h, i, r * 8 : (r + 1) * 8, :] = out[:, i * value_size : (i + 1) * value_size]

        for i in range(share):
            n = h * share + i
            heads = slice(n * value_size, (n + 1) * value_size)
            part = [
                right_buf[h, i, pl.ds(2 * j, rows, stride=8), :]
                + right_buf[h, i, pl.ds(2 * j + 1, rows, stride=8), :]
                for j in range(4)
            ]
            d0, d1 = decays[0][:, n : n + 1], decays[1][:, n : n + 1]
            b0, b1 = betas[0][:, n : n + 1], betas[1][:, n : n + 1]
            u0 = b0 * (value_all[:, 0, heads] - d0 * part[0])
            o0 = d0 * part[1] + key_query00 * u0
            u1 = b1 * (value_all[:, 1, heads] - d1 * (d0 * part[2] + key_key * u0))
            o1 = d1 * (d0 * part[3] + key_query01 * u0) + key_query11 * u1
            for p, o in enumerate((o0, o1)):
                g = gate_all[:, p, heads]
                mean = jnp.mean(o * o, axis=-1, keepdims=True)
                mixed[p].append(
                    o * lax.rsqrt(mean + eps_norm) * gain * (g / (1.0 + jnp.exp(-g)))
                )

    mixer_out = jnp.concatenate(
        [jnp.concatenate(mixed[p], axis=-1) for p in range(2)], axis=0
    ).astype(bf16)
    for copy in late:
        copy.wait()
    tokens, extra = 2 * rows, routed_ref.shape[1] - proj_hbm.shape[1]
    ids = jnp.concatenate([ids_ref[:, p, :] for p in range(2)], axis=0)
    lane = lax.broadcasted_iota(jnp.int32, (tokens, extra), 1)
    chosen = jnp.zeros((tokens, extra), f32)
    for k in range(ids.shape[1]):
        chosen = chosen + (ids[:, k : k + 1] == lane).astype(f32)
    routed_ref[:, -extra:] = chosen.astype(bf16)
    hidden = hidden_ref[...].astype(f32)
    total = jnp.concatenate([hidden[:, p, :] for p in range(2)], axis=0)
    for c in range(chunks):
        proj_copy(c).wait()
        part = slice(c * depth, (c + 1) * depth)
        total = total + jnp.dot(mixer_out[:, part], proj_buf[part, :], preferred_element_type=f32)
    middle = total.astype(bf16)
    middle_ref[...] = middle
    wide = middle.astype(f32)
    routed = (
        wide
        * lax.rsqrt(jnp.mean(wide * wide, axis=-1, keepdims=True) + eps_norm)
        * post_gain_ref[...].reshape(1, wide.shape[1])
    ).astype(bf16)
    routed_ref[:, : routed.shape[1]] = routed


def choice_place(experts, piece):
    per = max(1, 128 // experts)
    return piece // per, piece % per * experts


def column_kernel(experts, *refs):
    out_ref = refs[-1]
    pieces = refs[:-1]
    tokens = pieces[0].shape[0]
    width = pieces[0].shape[1] - 128
    column = tokens * len(pieces)
    for i, ref in enumerate(pieces):
        for j in range(width // 128):
            first = j * column + i * tokens
            out_ref[first : first + tokens, :] = ref[:, j * 128 : (j + 1) * 128]
    groups = {}
    for i, ref in enumerate(pieces):
        group, start = choice_place(experts, i)
        choices = ref[:, width:].astype(f32)
        if start:
            choices = pltpu.roll(choices, start, 1)
        groups[group] = choices + groups.get(group, 0.0)
    first = column * (width // 128)
    for group, choices in groups.items():
        out_ref[first + group * tokens : first + (group + 1) * tokens, :] = choices.astype(bf16)


def expert_kernel(tokens, count, *refs):
    blocks = refs[:count]
    router, up_own, down_own, up_other, down_other = refs[count : count + 5]
    outs = refs[count + 5 :]
    rows, width = outs[0].shape
    hidden_units = down_own.shape[1]
    me = lax.axis_index("dp")
    experts = router.shape[0]
    blocks_rows, blocks_chosen = [], []
    for block in blocks:
        parts = [block[j * rows : (j + 1) * rows, :] for j in range(width // 128)]
        blocks_rows.append(jnp.concatenate(parts, axis=-1))
        for i in range(rows // tokens):
            group, start = choice_place(experts, i)
            first = rows * (width // 128) + group * tokens
            choices = block[first : first + tokens, :].astype(f32)
            if start:
                choices = pltpu.roll(choices, 128 - start, 1)
            blocks_chosen.append(choices[:, :experts])
    x = jnp.concatenate(blocks_rows, axis=0)
    chosen = jnp.concatenate(blocks_chosen, axis=0) > 0.0
    raised = jnp.where(chosen, jnp.exp(nt_dot(x, router[...])), 0.0)
    whole = jnp.sum(raised, axis=-1, keepdims=True)
    lane = lax.broadcasted_iota(jnp.int32, raised.shape, 1)
    total = None
    for up_ref, down_ref, e in ((up_own, down_own, me), (up_other, down_other, me ^ 1)):
        both = jnp.dot(x, up_ref[0], preferred_element_type=f32)
        g = both[:, :hidden_units]
        activated = (g / (1.0 + jnp.exp(-g)) * both[:, hidden_units:]).astype(bf16)
        result = jnp.dot(activated, down_ref[0], preferred_element_type=f32).astype(bf16)
        share = jnp.sum(jnp.where(lane == e, raised, 0.0), axis=-1, keepdims=True) / whole
        part = share * result.astype(f32)
        total = part if total is None else total + part
    for i, out in enumerate(outs):
        out[...] = total[i * rows : (i + 1) * rows].astype(out.dtype)


def column_sum_kernel(tokens, *refs):
    own_ref = refs[0]
    count = (own_ref.shape[0] // tokens)
    outs = refs[-count:]
    total = own_ref[...]
    for ref in refs[1:-count]:
        total = total + ref[...].astype(f32)
    for i, out in enumerate(outs):
        out[...] = total[i * tokens : (i + 1) * tokens].astype(out.dtype)


def final_kernel(*refs):
    out_ref = refs[-1]
    rows = out_ref.shape[0]
    total = refs[0][...].astype(f32) + refs[1][...]
    for ref in refs[2:-1]:
        total = total + ref[...].astype(f32)
    total = total.astype(bf16)
    for p in range(2):
        out_ref[:, p, :] = total[p * rows : (p + 1) * rows]


def chip_masks(device_count):
    bits = device_count.bit_length() - 2
    low = bits // 2
    near = [m << 1 for m in range(1, 1 << low)]
    far = [m << (1 + low) for m in range(1, 1 << (bits - low))]
    if len(near) != len(far):
        return list(zip(far, far)), list(zip(near, near))
    return list(zip(far, near)), list(zip(near, far))


def hop(x, masks):
    count = lax.axis_size("dp")
    return lax.ppermute(x, "dp", [(i, i ^ masks[i % 2]) for i in range(count)])


def vmem(count):
    return [pl.BlockSpec(memory_space=pltpu.VMEM)] * count


def shards(
    hidden_in,
    query_in,
    key_in,
    value_in,
    gate_in,
    decay_in,
    beta_in,
    decay_log,
    step_bias,
    norm_gain,
    state_in,
    out_proj,
    post_gain,
    router_weight,
    expert_gate_up,
    expert_down,
    expert_ids,
):
    device_count = lax.axis_size("dp")
    expert_total = expert_gate_up.shape[0] * device_count
    row_count, _, model_width = hidden_in.shape
    value_heads, key_size, value_size = state_in.shape[1:]
    key_heads = query_in.shape[2] // key_size
    share = value_heads // key_heads
    token_count = row_count * 2
    sent_width = model_width + 128
    first, second = chip_masks(device_count)
    chunks = 2
    params = pltpu.CompilerParams(vmem_limit_bytes=48 * 1024 * 1024)
    operands = (
        hidden_in,
        query_in,
        key_in,
        value_in,
        gate_in,
        decay_in,
        beta_in,
        decay_log,
        step_bias,
        norm_gain,
        post_gain,
        expert_ids,
        state_in,
        out_proj,
    )
    operands = [pltpu.with_memory_space_constraint(x, pltpu.HBM) for x in operands]
    up_other, down_other = hop(expert_gate_up, (1, 1)), hop(expert_down, (1, 1))
    routed, middle = pl.pallas_call(
        mixer_kernel,
        out_shape=(
            jax.ShapeDtypeStruct((token_count, sent_width), bf16),
            jax.ShapeDtypeStruct((token_count, model_width), bf16),
        ),
        in_specs=[pl.BlockSpec(memory_space=pltpu.HBM)] * len(operands),
        out_specs=tuple(vmem(2)),
        scratch_shapes=[pltpu.VMEM(x.shape, x.dtype) for x in operands[:12]]
        + [
            pltpu.VMEM(state_in.shape, bf16),
            pltpu.VMEM(out_proj.shape, bf16),
            pltpu.VMEM((key_heads, 8 * row_count, key_size), f32),
            pltpu.VMEM((key_heads, share, 8 * row_count, value_size), f32),
            pltpu.SemaphoreType.DMA((12,)),
            pltpu.SemaphoreType.DMA((key_heads // 2,)),
            pltpu.SemaphoreType.DMA((chunks,)),
        ],
        compiler_params=params,
        name="mixer",
    )(*operands)

    def local(body, name, outs, *args):
        return pl.pallas_call(
            body,
            out_shape=tuple(jax.ShapeDtypeStruct(*o) for o in outs),
            in_specs=vmem(len(args)),
            out_specs=tuple(vmem(len(outs))),
            compiler_params=params,
            name=name,
        )(*args)

    weights = (router_weight.T, expert_gate_up, expert_down, up_other, down_other)
    column_rows = token_count * (len(first) + 1)
    groups = choice_place(expert_total, len(first))[0] + 1
    column_size = column_rows * (model_width // 128) + groups * token_count
    pieces = [hop(routed, m) for m in first]
    (column,) = local(
        functools.partial(column_kernel, expert_total),
        "column",
        [((column_size, 128), bf16)],
        routed,
        *pieces,
    )
    columns = [hop(column, m) for m in second]
    (own,) = local(
        functools.partial(expert_kernel, token_count, 1),
        "own_experts",
        [((column_rows, model_width), f32)],
        column,
        *weights,
    )
    results = local(
        functools.partial(expert_kernel, token_count, len(second)),
        "experts",
        [((column_rows, model_width), bf16)] * len(second),
        *columns,
        *weights,
    )
    back = [hop(r, m) for r, m in zip(results[::-1], second[::-1])]
    mine, *others = local(
        functools.partial(column_sum_kernel, token_count),
        "column_sum",
        [((token_count, model_width), f32)] + [((token_count, model_width), bf16)] * len(first),
        own,
        *back,
    )
    home = [hop(r, m) for r, m in zip(others[::-1], first[::-1])]
    (out,) = local(final_kernel, "final", [(hidden_in.shape, bf16)], middle, mine, *home)
    return out


def solution(mesh):
    rows = P(("groups", "dp"))
    placed = (
        (rows,) * 7 + (P(),) * 3 + (rows,) + (P(),) * 3 + (P("dp"),) * 2 + (rows,)
    )
    return jax.shard_map(
        shards,
        mesh=mesh,
        in_specs=placed,
        out_specs=rows,
        check_vma=False,
    )
```

```python
import functools

import jax
import jax.numpy as jnp
from jax import lax
from jax.experimental import pallas as pl
from jax.experimental.pallas import tpu as pltpu
from jax.sharding import PartitionSpec as P

eps_norm = 1e-06
f32 = jnp.float32
bf16 = jnp.bfloat16


def nt_dot(a, b):
    return lax.dot_general(a, b, (((1,), (1,)), ((), ())), preferred_element_type=f32)


def mixer_kernel(
    hidden_hbm,
    query_hbm,
    key_hbm,
    value_hbm,
    gate_hbm,
    decay_in_hbm,
    beta_in_hbm,
    decay_log_hbm,
    step_bias_hbm,
    norm_gain_hbm,
    post_gain_hbm,
    ids_hbm,
    state_hbm,
    proj_hbm,
    routed_ref,
    middle_ref,
    hidden_ref,
    query_ref,
    key_ref,
    value_ref,
    gate_ref,
    decay_in_ref,
    beta_in_ref,
    decay_log_ref,
    step_bias_ref,
    norm_gain_ref,
    post_gain_ref,
    ids_ref,
    state_buf,
    proj_buf,
    left_buf,
    right_buf,
    small_sem,
    state_sem,
    proj_sem,
):
    rows = query_ref.shape[0]
    value_heads, key_size, value_size = state_hbm.shape[1:]
    key_heads = query_ref.shape[2] // key_size
    share = value_heads // key_heads
    span = share * value_size
    chunks = proj_sem.shape[0]
    depth = proj_hbm.shape[0] // chunks

    groups = state_sem.shape[0]
    group = key_heads // groups

    def state_copy(c):
        part = pl.ds(c * group * share, group * share)
        return pltpu.make_async_copy(
            state_hbm.at[:, part], state_buf.at[:, part], state_sem.at[c]
        )

    def proj_copy(c):
        part = pl.ds(c * depth, depth)
        return pltpu.make_async_copy(proj_hbm.at[part], proj_buf.at[part], proj_sem.at[c])

    pairs = (
        (key_hbm, key_ref),
        (query_hbm, query_ref),
        (decay_log_hbm, decay_log_ref),
        (step_bias_hbm, step_bias_ref),
        (decay_in_hbm, decay_in_ref),
        (beta_in_hbm, beta_in_ref),
        (norm_gain_hbm, norm_gain_ref),
        (value_hbm, value_ref),
        (gate_hbm, gate_ref),
        (ids_hbm, ids_ref),
        (hidden_hbm, hidden_ref),
        (post_gain_hbm, post_gain_ref),
    )
    small = [pltpu.make_async_copy(a, b, small_sem.at[i]) for i, (a, b) in enumerate(pairs)]
    early, late = small[:9], small[9:]
    for copy in early[:2]:
        copy.start()
    state_copy(0).start()
    for copy in early[2:]:
        copy.start()
    for c in range(1, groups):
        state_copy(c).start()
    for c in range(chunks):
        proj_copy(c).start()
    for copy in late:
        copy.start()
    for copy in early:
        copy.wait()

    query_all = query_ref[...].astype(f32)
    key_all = key_ref[...].astype(f32)
    value_all = value_ref[...].astype(f32)
    gate_all = gate_ref[...].astype(f32)
    decay_in = decay_in_ref[...].astype(f32)
    beta_in = beta_in_ref[...].astype(f32)
    rate = -jnp.exp(decay_log_ref[...].reshape(1, value_heads))
    bias = step_bias_ref[...].reshape(1, value_heads)
    decays, betas = [], []
    for p in range(2):
        decays.append(jnp.exp(rate * jax.nn.softplus(decay_in[:, p, :] + bias)))
        betas.append(1.0 / (1.0 + jnp.exp(-beta_in[:, p, :])))
    gain = norm_gain_ref[...].reshape(1, value_size)

    mixed = [[], []]
    for h in range(key_heads):
        lanes = slice(h * key_size, (h + 1) * key_size)
        keys, queries = [], []
        for p in range(2):
            k = key_all[:, p, lanes]
            q = query_all[:, p, lanes]
            keys.append(k * lax.rsqrt(jnp.sum(k * k, axis=-1, keepdims=True) + eps_norm))
            queries.append(
                q
                * lax.rsqrt(jnp.sum(q * q, axis=-1, keepdims=True) + eps_norm)
                * key_size ** (-0.5)
            )
        vectors = (keys[0], queries[0], keys[1], queries[1])
        for j, v in enumerate(vectors):
            high = v.astype(bf16).astype(f32)
            left_buf[h, pl.ds(2 * j, rows, stride=8), :] = high
            left_buf[h, pl.ds(2 * j + 1, rows, stride=8), :] = v - high
        key_key = jnp.sum(keys[0] * keys[1], axis=-1, keepdims=True)
        key_query00 = jnp.sum(keys[0] * queries[0], axis=-1, keepdims=True)
        key_query01 = jnp.sum(keys[0] * queries[1], axis=-1, keepdims=True)
        key_query11 = jnp.sum(keys[1] * queries[1], axis=-1, keepdims=True)

        if h % group == 0:
            state_copy(h // group).wait()
        for r in range(rows):
            left = left_buf[h, r * 8 : (r + 1) * 8, :].astype(bf16)
            right = jnp.concatenate([state_buf[r, h * share + i] for i in range(share)], axis=-1)
            out = jnp.dot(left, right, preferred_element_type=f32)
            for i in range(share):
                right_buf[h, i, r * 8 : (r + 1) * 8, :] = out[:, i * value_size : (i + 1) * value_size]

        for i in range(share):
            n = h * share + i
            heads = slice(n * value_size, (n + 1) * value_size)
            part = [
                right_buf[h, i, pl.ds(2 * j, rows, stride=8), :]
                + right_buf[h, i, pl.ds(2 * j + 1, rows, stride=8), :]
                for j in range(4)
            ]
            d0, d1 = decays[0][:, n : n + 1], decays[1][:, n : n + 1]
            b0, b1 = betas[0][:, n : n + 1], betas[1][:, n : n + 1]
            u0 = b0 * (value_all[:, 0, heads] - d0 * part[0])
            o0 = d0 * part[1] + key_query00 * u0
            u1 = b1 * (value_all[:, 1, heads] - d1 * (d0 * part[2] + key_key * u0))
            o1 = d1 * (d0 * part[3] + key_query01 * u0) + key_query11 * u1
            for p, o in enumerate((o0, o1)):
                g = gate_all[:, p, heads]
                mean = jnp.mean(o * o, axis=-1, keepdims=True)
                mixed[p].append(
                    o * lax.rsqrt(mean + eps_norm) * gain * (g / (1.0 + jnp.exp(-g)))
                )

    mixer_out = jnp.concatenate(
        [jnp.concatenate(mixed[p], axis=-1) for p in range(2)], axis=0
    ).astype(bf16)
    for copy in late:
        copy.wait()
    tokens, extra = 2 * rows, routed_ref.shape[1] - proj_hbm.shape[1]
    ids = jnp.concatenate([ids_ref[:, p, :] for p in range(2)], axis=0)
    lane = lax.broadcasted_iota(jnp.int32, (tokens, extra), 1)
    chosen = jnp.zeros((tokens, extra), f32)
    for k in range(ids.shape[1]):
        chosen = chosen + (ids[:, k : k + 1] == lane).astype(f32)
    routed_ref[:, -extra:] = chosen.astype(bf16)
    hidden = hidden_ref[...].astype(f32)
    total = jnp.concatenate([hidden[:, p, :] for p in range(2)], axis=0)
    for c in range(chunks):
        proj_copy(c).wait()
        part = slice(c * depth, (c + 1) * depth)
        total = total + jnp.dot(mixer_out[:, part], proj_buf[part, :], preferred_element_type=f32)
    middle = total.astype(bf16)
    middle_ref[...] = middle
    wide = middle.astype(f32)
    routed = (
        wide
        * lax.rsqrt(jnp.mean(wide * wide, axis=-1, keepdims=True) + eps_norm)
        * post_gain_ref[...].reshape(1, wide.shape[1])
    ).astype(bf16)
    routed_ref[:, : routed.shape[1]] = routed


def choice_place(experts, piece):
    per = max(1, 128 // experts)
    return piece // per, piece % per * experts


def column_kernel(experts, *refs):
    out_ref = refs[-1]
    pieces = refs[:-1]
    tokens = pieces[0].shape[0]
    width = pieces[0].shape[1] - 128
    column = tokens * len(pieces)
    for i, ref in enumerate(pieces):
        for j in range(width // 128):
            first = j * column + i * tokens
            out_ref[first : first + tokens, :] = ref[:, j * 128 : (j + 1) * 128]
    groups = {}
    for i, ref in enumerate(pieces):
        group, start = choice_place(experts, i)
        choices = ref[:, width:].astype(f32)
        if start:
            choices = pltpu.roll(choices, start, 1)
        groups[group] = choices + groups.get(group, 0.0)
    first = column * (width // 128)
    for group, choices in groups.items():
        out_ref[first + group * tokens : first + (group + 1) * tokens, :] = choices.astype(bf16)


def expert_kernel(tokens, count, *refs):
    blocks = refs[:count]
    router, up_own, down_own, up_other, down_other = refs[count : count + 5]
    outs = refs[count + 5 :]
    rows, width = outs[0].shape
    hidden_units = down_own.shape[1]
    me = lax.axis_index("dp")
    experts = router.shape[0]
    blocks_rows, blocks_chosen = [], []
    for block in blocks:
        parts = [block[j * rows : (j + 1) * rows, :] for j in range(width // 128)]
        blocks_rows.append(jnp.concatenate(parts, axis=-1))
        for i in range(rows // tokens):
            group, start = choice_place(experts, i)
            first = rows * (width // 128) + group * tokens
            choices = block[first : first + tokens, :].astype(f32)
            if start:
                choices = pltpu.roll(choices, 128 - start, 1)
            blocks_chosen.append(choices[:, :experts])
    x = jnp.concatenate(blocks_rows, axis=0)
    chosen = jnp.concatenate(blocks_chosen, axis=0) > 0.0
    raised = jnp.where(chosen, jnp.exp(nt_dot(x, router[...])), 0.0)
    whole = jnp.sum(raised, axis=-1, keepdims=True)
    lane = lax.broadcasted_iota(jnp.int32, raised.shape, 1)
    total = None
    for up_ref, down_ref, e in ((up_own, down_own, me), (up_other, down_other, me ^ 1)):
        both = jnp.dot(x, up_ref[0], preferred_element_type=f32)
        g = both[:, :hidden_units]
        activated = (g / (1.0 + jnp.exp(-g)) * both[:, hidden_units:]).astype(bf16)
        result = jnp.dot(activated, down_ref[0], preferred_element_type=f32).astype(bf16)
        share = jnp.sum(jnp.where(lane == e, raised, 0.0), axis=-1, keepdims=True) / whole
        part = share * result.astype(f32)
        total = part if total is None else total + part
    for i, out in enumerate(outs):
        out[...] = total[i * rows : (i + 1) * rows].astype(out.dtype)


def column_sum_kernel(tokens, *refs):
    own_ref = refs[0]
    count = (own_ref.shape[0] // tokens)
    outs = refs[-count:]
    total = own_ref[...]
    for ref in refs[1:-count]:
        total = total + ref[...].astype(f32)
    for i, out in enumerate(outs):
        out[...] = total[i * tokens : (i + 1) * tokens].astype(out.dtype)


def final_kernel(*refs):
    out_ref = refs[-1]
    rows = out_ref.shape[0]
    total = refs[0][...].astype(f32) + refs[1][...]
    for ref in refs[2:-1]:
        total = total + ref[...].astype(f32)
    total = total.astype(bf16)
    for p in range(2):
        out_ref[:, p, :] = total[p * rows : (p + 1) * rows]


def chip_masks(device_count):
    bits = device_count.bit_length() - 2
    low = bits // 2
    near = [m << 1 for m in range(1, 1 << low)]
    far = [m << (1 + low) for m in range(1, 1 << (bits - low))]
    if len(near) != len(far):
        return list(zip(far, far)), list(zip(near, near))
    turned = [near[1], near[0], *near[2:]]
    return list(zip(far, near)), list(zip(turned, far))


def hop(x, masks):
    count = lax.axis_size("dp")
    return lax.ppermute(x, "dp", [(i, i ^ masks[i % 2]) for i in range(count)])


def vmem(count):
    return [pl.BlockSpec(memory_space=pltpu.VMEM)] * count


def shards(
    hidden_in,
    query_in,
    key_in,
    value_in,
    gate_in,
    decay_in,
    beta_in,
    decay_log,
    step_bias,
    norm_gain,
    state_in,
    out_proj,
    post_gain,
    router_weight,
    expert_gate_up,
    expert_down,
    expert_ids,
):
    device_count = lax.axis_size("dp")
    expert_total = expert_gate_up.shape[0] * device_count
    row_count, _, model_width = hidden_in.shape
    value_heads, key_size, value_size = state_in.shape[1:]
    key_heads = query_in.shape[2] // key_size
    share = value_heads // key_heads
    token_count = row_count * 2
    sent_width = model_width + 128
    first, second = chip_masks(device_count)
    chunks = 2
    params = pltpu.CompilerParams(vmem_limit_bytes=48 * 1024 * 1024)
    operands = (
        hidden_in,
        query_in,
        key_in,
        value_in,
        gate_in,
        decay_in,
        beta_in,
        decay_log,
        step_bias,
        norm_gain,
        post_gain,
        expert_ids,
        state_in,
        out_proj,
    )
    operands = [pltpu.with_memory_space_constraint(x, pltpu.HBM) for x in operands]
    up_other, down_other = hop(expert_gate_up, (1, 1)), hop(expert_down, (1, 1))
    routed, middle = pl.pallas_call(
        mixer_kernel,
        out_shape=(
            jax.ShapeDtypeStruct((token_count, sent_width), bf16),
            jax.ShapeDtypeStruct((token_count, model_width), bf16),
        ),
        in_specs=[pl.BlockSpec(memory_space=pltpu.HBM)] * len(operands),
        out_specs=tuple(vmem(2)),
        scratch_shapes=[pltpu.VMEM(x.shape, x.dtype) for x in operands[:12]]
        + [
            pltpu.VMEM(state_in.shape, bf16),
            pltpu.VMEM(out_proj.shape, bf16),
            pltpu.VMEM((key_heads, 8 * row_count, key_size), f32),
            pltpu.VMEM((key_heads, share, 8 * row_count, value_size), f32),
            pltpu.SemaphoreType.DMA((12,)),
            pltpu.SemaphoreType.DMA((key_heads // 2,)),
            pltpu.SemaphoreType.DMA((chunks,)),
        ],
        compiler_params=params,
        name="mixer",
    )(*operands)

    def local(body, name, outs, *args):
        return pl.pallas_call(
            body,
            out_shape=tuple(jax.ShapeDtypeStruct(*o) for o in outs),
            in_specs=vmem(len(args)),
            out_specs=tuple(vmem(len(outs))),
            compiler_params=params,
            name=name,
        )(*args)

    weights = (router_weight.T, expert_gate_up, expert_down, up_other, down_other)
    column_rows = token_count * (len(first) + 1)
    groups = choice_place(expert_total, len(first))[0] + 1
    column_size = column_rows * (model_width // 128) + groups * token_count
    pieces = [hop(routed, m) for m in first]
    (column,) = local(
        functools.partial(column_kernel, expert_total),
        "column",
        [((column_size, 128), bf16)],
        routed,
        *pieces,
    )
    columns = [hop(column, m) for m in second]
    (own,) = local(
        functools.partial(expert_kernel, token_count, 1),
        "own_experts",
        [((column_rows, model_width), f32)],
        column,
        *weights,
    )
    results = local(
        functools.partial(expert_kernel, token_count, len(second)),
        "experts",
        [((column_rows, model_width), bf16)] * len(second),
        *columns,
        *weights,
    )
    back = [hop(r, m) for r, m in zip(results[::-1], second[::-1])]
    mine, *others = local(
        functools.partial(column_sum_kernel, token_count),
        "column_sum",
        [((token_count, model_width), f32)] + [((token_count, model_width), bf16)] * len(first),
        own,
        *back,
    )
    home = [hop(r, m) for r, m in zip(others[::-1], first[::-1])]
    (out,) = local(final_kernel, "final", [(hidden_in.shape, bf16)], middle, mine, *home)
    return out


def solution(mesh):
    rows = P(("groups", "dp"))
    placed = (
        (rows,) * 7 + (P(),) * 3 + (rows,) + (P(),) * 3 + (P("dp"),) * 2 + (rows,)
    )
    return jax.shard_map(
        shards,
        mesh=mesh,
        in_specs=placed,
        out_specs=rows,
        check_vma=False,
    )
```

```python
import functools

import jax
import jax.numpy as jnp
from jax import lax
from jax.experimental import pallas as pl
from jax.experimental.pallas import tpu as pltpu
from jax.sharding import PartitionSpec as P

eps_norm = 1e-06
f32 = jnp.float32
bf16 = jnp.bfloat16


def nt_dot(a, b):
    return lax.dot_general(a, b, (((1,), (1,)), ((), ())), preferred_element_type=f32)


def mixer_kernel(
    hidden_hbm,
    query_hbm,
    key_hbm,
    value_hbm,
    gate_hbm,
    decay_in_hbm,
    beta_in_hbm,
    decay_log_hbm,
    step_bias_hbm,
    norm_gain_hbm,
    post_gain_hbm,
    ids_hbm,
    state_hbm,
    proj_hbm,
    routed_ref,
    middle_ref,
    hidden_ref,
    query_ref,
    key_ref,
    value_ref,
    gate_ref,
    decay_in_ref,
    beta_in_ref,
    decay_log_ref,
    step_bias_ref,
    norm_gain_ref,
    post_gain_ref,
    ids_ref,
    state_buf,
    proj_buf,
    left_buf,
    right_buf,
    small_sem,
    state_sem,
    proj_sem,
):
    rows = query_ref.shape[0]
    value_heads, key_size, value_size = state_hbm.shape[1:]
    key_heads = query_ref.shape[2] // key_size
    share = value_heads // key_heads
    span = share * value_size
    chunks = proj_sem.shape[0]
    cut = proj_hbm.shape[0] // 2

    groups = state_sem.shape[0]
    group = key_heads // groups

    def state_copy(c):
        part = pl.ds(c * group * share, group * share)
        return pltpu.make_async_copy(
            state_hbm.at[:, part], state_buf.at[:, part], state_sem.at[c]
        )

    def proj_copy(c):
        part = pl.ds(c * cut, cut)
        return pltpu.make_async_copy(proj_hbm.at[part], proj_buf.at[part], proj_sem.at[c])

    pairs = (
        (key_hbm, key_ref),
        (query_hbm, query_ref),
        (decay_log_hbm, decay_log_ref),
        (step_bias_hbm, step_bias_ref),
        (decay_in_hbm, decay_in_ref),
        (beta_in_hbm, beta_in_ref),
        (norm_gain_hbm, norm_gain_ref),
        (value_hbm, value_ref),
        (gate_hbm, gate_ref),
        (ids_hbm, ids_ref),
        (hidden_hbm, hidden_ref),
        (post_gain_hbm, post_gain_ref),
    )
    small = [pltpu.make_async_copy(a, b, small_sem.at[i]) for i, (a, b) in enumerate(pairs)]
    early, late = small[:9], small[9:]
    for copy in early[:2]:
        copy.start()
    state_copy(0).start()
    for copy in early[2:]:
        copy.start()
    for c in range(1, groups):
        state_copy(c).start()
    for copy in late:
        copy.start()
    for c in range(chunks):
        proj_copy(c).start()
    for copy in early:
        copy.wait()

    query_all = query_ref[...].astype(f32)
    key_all = key_ref[...].astype(f32)
    value_all = value_ref[...].astype(f32)
    gate_all = gate_ref[...].astype(f32)
    decay_in = decay_in_ref[...].astype(f32)
    beta_in = beta_in_ref[...].astype(f32)
    rate = -jnp.exp(decay_log_ref[...].reshape(1, value_heads))
    bias = step_bias_ref[...].reshape(1, value_heads)
    decays, betas = [], []
    for p in range(2):
        decays.append(jnp.exp(rate * jax.nn.softplus(decay_in[:, p, :] + bias)))
        betas.append(1.0 / (1.0 + jnp.exp(-beta_in[:, p, :])))
    gain = norm_gain_ref[...].reshape(1, value_size)

    def joined(lists):
        return jnp.concatenate([jnp.concatenate(m, axis=-1) for m in lists], axis=0).astype(bf16)

    half = value_heads // 2
    mixed = [[], []]
    total = None
    for h in range(key_heads):
        if h == key_heads // 2:
            for copy in late:
                copy.wait()
            tokens, extra = 2 * rows, routed_ref.shape[1] - proj_hbm.shape[1]
            ids = jnp.concatenate([ids_ref[:, p, :] for p in range(2)], axis=0)
            lane = lax.broadcasted_iota(jnp.int32, (tokens, extra), 1)
            chosen = jnp.zeros((tokens, extra), f32)
            for k in range(ids.shape[1]):
                chosen = chosen + (ids[:, k : k + 1] == lane).astype(f32)
            routed_ref[:, -extra:] = chosen.astype(bf16)
        lanes = slice(h * key_size, (h + 1) * key_size)
        keys, queries = [], []
        for p in range(2):
            k = key_all[:, p, lanes]
            q = query_all[:, p, lanes]
            keys.append(k * lax.rsqrt(jnp.sum(k * k, axis=-1, keepdims=True) + eps_norm))
            queries.append(
                q
                * lax.rsqrt(jnp.sum(q * q, axis=-1, keepdims=True) + eps_norm)
                * key_size ** (-0.5)
            )
        vectors = (keys[0], queries[0], keys[1], queries[1])
        for j, v in enumerate(vectors):
            high = v.astype(bf16).astype(f32)
            left_buf[h, pl.ds(2 * j, rows, stride=8), :] = high
            left_buf[h, pl.ds(2 * j + 1, rows, stride=8), :] = v - high
        key_key = jnp.sum(keys[0] * keys[1], axis=-1, keepdims=True)
        key_query00 = jnp.sum(keys[0] * queries[0], axis=-1, keepdims=True)
        key_query01 = jnp.sum(keys[0] * queries[1], axis=-1, keepdims=True)
        key_query11 = jnp.sum(keys[1] * queries[1], axis=-1, keepdims=True)

        if h % group == 0:
            state_copy(h // group).wait()
            if h == key_heads - group:
                proj_copy(0).wait()
                total = jnp.dot(
                    joined([m[:half] for m in mixed]), proj_buf[:cut, :], preferred_element_type=f32
                )
        for r in range(rows):
            left = left_buf[h, r * 8 : (r + 1) * 8, :].astype(bf16)
            right = jnp.concatenate([state_buf[r, h * share + i] for i in range(share)], axis=-1)
            out = jnp.dot(left, right, preferred_element_type=f32)
            for i in range(share):
                right_buf[h, i, r * 8 : (r + 1) * 8, :] = out[:, i * value_size : (i + 1) * value_size]

        for i in range(share):
            n = h * share + i
            heads = slice(n * value_size, (n + 1) * value_size)
            part = [
                right_buf[h, i, pl.ds(2 * j, rows, stride=8), :]
                + right_buf[h, i, pl.ds(2 * j + 1, rows, stride=8), :]
                for j in range(4)
            ]
            d0, d1 = decays[0][:, n : n + 1], decays[1][:, n : n + 1]
            b0, b1 = betas[0][:, n : n + 1], betas[1][:, n : n + 1]
            u0 = b0 * (value_all[:, 0, heads] - d0 * part[0])
            o0 = d0 * part[1] + key_query00 * u0
            u1 = b1 * (value_all[:, 1, heads] - d1 * (d0 * part[2] + key_key * u0))
            o1 = d1 * (d0 * part[3] + key_query01 * u0) + key_query11 * u1
            for p, o in enumerate((o0, o1)):
                g = gate_all[:, p, heads]
                mean = jnp.mean(o * o, axis=-1, keepdims=True)
                mixed[p].append(
                    o * lax.rsqrt(mean + eps_norm) * gain * (g / (1.0 + jnp.exp(-g)))
                )

    hidden = hidden_ref[...].astype(f32)
    total = total + jnp.concatenate([hidden[:, p, :] for p in range(2)], axis=0)
    proj_copy(1).wait()
    total = total + jnp.dot(
        joined([m[half:] for m in mixed]), proj_buf[cut:, :], preferred_element_type=f32
    )
    middle = total.astype(bf16)
    middle_ref[...] = middle
    wide = middle.astype(f32)
    routed = (
        wide
        * lax.rsqrt(jnp.mean(wide * wide, axis=-1, keepdims=True) + eps_norm)
        * post_gain_ref[...].reshape(1, wide.shape[1])
    ).astype(bf16)
    routed_ref[:, : routed.shape[1]] = routed


def choice_place(experts, piece):
    per = max(1, 128 // experts)
    return piece // per, piece % per * experts


def column_kernel(experts, *refs):
    out_ref = refs[-1]
    pieces = refs[:-1]
    tokens = pieces[0].shape[0]
    width = pieces[0].shape[1] - 128
    column = tokens * len(pieces)
    for i, ref in enumerate(pieces):
        for j in range(width // 128):
            first = j * column + i * tokens
            out_ref[first : first + tokens, :] = ref[:, j * 128 : (j + 1) * 128]
    groups = {}
    for i, ref in enumerate(pieces):
        group, start = choice_place(experts, i)
        choices = ref[:, width:].astype(f32)
        if start:
            choices = pltpu.roll(choices, start, 1)
        groups[group] = choices + groups.get(group, 0.0)
    first = column * (width // 128)
    for group, choices in groups.items():
        out_ref[first + group * tokens : first + (group + 1) * tokens, :] = choices.astype(bf16)


def expert_kernel(tokens, count, *refs):
    blocks = refs[:count]
    router, up_own, down_own, up_other, down_other = refs[count : count + 5]
    outs = refs[count + 5 :]
    rows, width = outs[0].shape
    hidden_units = down_own.shape[1]
    me = lax.axis_index("dp")
    experts = router.shape[0]
    blocks_rows, blocks_chosen = [], []
    for block in blocks:
        parts = [block[j * rows : (j + 1) * rows, :] for j in range(width // 128)]
        blocks_rows.append(jnp.concatenate(parts, axis=-1))
        for i in range(rows // tokens):
            group, start = choice_place(experts, i)
            first = rows * (width // 128) + group * tokens
            choices = block[first : first + tokens, :].astype(f32)
            if start:
                choices = pltpu.roll(choices, 128 - start, 1)
            blocks_chosen.append(choices[:, :experts])
    x = jnp.concatenate(blocks_rows, axis=0)
    chosen = jnp.concatenate(blocks_chosen, axis=0) > 0.0
    raised = jnp.where(chosen, jnp.exp(nt_dot(x, router[...])), 0.0)
    whole = jnp.sum(raised, axis=-1, keepdims=True)
    lane = lax.broadcasted_iota(jnp.int32, raised.shape, 1)
    total = None
    for up_ref, down_ref, e in ((up_own, down_own, me), (up_other, down_other, me ^ 1)):
        both = jnp.dot(x, up_ref[0], preferred_element_type=f32)
        g = both[:, :hidden_units]
        activated = (g / (1.0 + jnp.exp(-g)) * both[:, hidden_units:]).astype(bf16)
        result = jnp.dot(activated, down_ref[0], preferred_element_type=f32).astype(bf16)
        share = jnp.sum(jnp.where(lane == e, raised, 0.0), axis=-1, keepdims=True) / whole
        part = share * result.astype(f32)
        total = part if total is None else total + part
    for i, out in enumerate(outs):
        out[...] = total[i * rows : (i + 1) * rows].astype(out.dtype)


def column_sum_kernel(tokens, *refs):
    own_ref = refs[0]
    count = (own_ref.shape[0] // tokens)
    outs = refs[-count:]
    total = own_ref[...]
    for ref in refs[1:-count]:
        total = total + ref[...].astype(f32)
    for i, out in enumerate(outs):
        out[...] = total[i * tokens : (i + 1) * tokens].astype(out.dtype)


def final_kernel(*refs):
    out_ref = refs[-1]
    rows = out_ref.shape[0]
    total = refs[0][...].astype(f32) + refs[1][...]
    for ref in refs[2:-1]:
        total = total + ref[...].astype(f32)
    total = total.astype(bf16)
    for p in range(2):
        out_ref[:, p, :] = total[p * rows : (p + 1) * rows]


def chip_masks(device_count):
    bits = device_count.bit_length() - 2
    low = bits // 2
    near = [m << 1 for m in range(1, 1 << low)]
    far = [m << (1 + low) for m in range(1, 1 << (bits - low))]
    if len(near) != len(far):
        return list(zip(far, far)), list(zip(near, near))
    turned = [near[1], near[0], *near[2:]]
    return list(zip(far, near)), list(zip(turned, far))


def hop(x, masks):
    count = lax.axis_size("dp")
    return lax.ppermute(x, "dp", [(i, i ^ masks[i % 2]) for i in range(count)])


def vmem(count):
    return [pl.BlockSpec(memory_space=pltpu.VMEM)] * count


def shards(
    hidden_in,
    query_in,
    key_in,
    value_in,
    gate_in,
    decay_in,
    beta_in,
    decay_log,
    step_bias,
    norm_gain,
    state_in,
    out_proj,
    post_gain,
    router_weight,
    expert_gate_up,
    expert_down,
    expert_ids,
):
    device_count = lax.axis_size("dp")
    expert_total = expert_gate_up.shape[0] * device_count
    row_count, _, model_width = hidden_in.shape
    value_heads, key_size, value_size = state_in.shape[1:]
    key_heads = query_in.shape[2] // key_size
    share = value_heads // key_heads
    token_count = row_count * 2
    sent_width = model_width + 128
    first, second = chip_masks(device_count)
    chunks = 2
    params = pltpu.CompilerParams(vmem_limit_bytes=48 * 1024 * 1024)
    operands = (
        hidden_in,
        query_in,
        key_in,
        value_in,
        gate_in,
        decay_in,
        beta_in,
        decay_log,
        step_bias,
        norm_gain,
        post_gain,
        expert_ids,
        state_in,
        out_proj,
    )
    operands = [pltpu.with_memory_space_constraint(x, pltpu.HBM) for x in operands]
    up_other, down_other = hop(expert_gate_up, (1, 1)), hop(expert_down, (1, 1))
    routed, middle = pl.pallas_call(
        mixer_kernel,
        out_shape=(
            jax.ShapeDtypeStruct((token_count, sent_width), bf16),
            jax.ShapeDtypeStruct((token_count, model_width), bf16),
        ),
        in_specs=[pl.BlockSpec(memory_space=pltpu.HBM)] * len(operands),
        out_specs=tuple(vmem(2)),
        scratch_shapes=[pltpu.VMEM(x.shape, x.dtype) for x in operands[:12]]
        + [
            pltpu.VMEM(state_in.shape, bf16),
            pltpu.VMEM(out_proj.shape, bf16),
            pltpu.VMEM((key_heads, 8 * row_count, key_size), f32),
            pltpu.VMEM((key_heads, share, 8 * row_count, value_size), f32),
            pltpu.SemaphoreType.DMA((12,)),
            pltpu.SemaphoreType.DMA((key_heads // 2,)),
            pltpu.SemaphoreType.DMA((chunks,)),
        ],
        compiler_params=params,
        name="mixer",
    )(*operands)

    def local(body, name, outs, *args):
        return pl.pallas_call(
            body,
            out_shape=tuple(jax.ShapeDtypeStruct(*o) for o in outs),
            in_specs=vmem(len(args)),
            out_specs=tuple(vmem(len(outs))),
            compiler_params=params,
            name=name,
        )(*args)

    weights = (router_weight.T, expert_gate_up, expert_down, up_other, down_other)
    column_rows = token_count * (len(first) + 1)
    groups = choice_place(expert_total, len(first))[0] + 1
    column_size = column_rows * (model_width // 128) + groups * token_count
    pieces = [hop(routed, m) for m in first]
    (column,) = local(
        functools.partial(column_kernel, expert_total),
        "column",
        [((column_size, 128), bf16)],
        routed,
        *pieces,
    )
    columns = [hop(column, m) for m in second]
    (own,) = local(
        functools.partial(expert_kernel, token_count, 1),
        "own_experts",
        [((column_rows, model_width), f32)],
        column,
        *weights,
    )
    results = local(
        functools.partial(expert_kernel, token_count, len(second)),
        "experts",
        [((column_rows, model_width), bf16)] * len(second),
        *columns,
        *weights,
    )
    back = [hop(r, m) for r, m in zip(results[::-1], second[::-1])]
    mine, *others = local(
        functools.partial(column_sum_kernel, token_count),
        "column_sum",
        [((token_count, model_width), f32)] + [((token_count, model_width), bf16)] * len(first),
        own,
        *back,
    )
    home = [hop(r, m) for r, m in zip(others[::-1], first[::-1])]
    (out,) = local(final_kernel, "final", [(hidden_in.shape, bf16)], middle, mine, *home)
    return out


def solution(mesh):
    rows = P(("groups", "dp"))
    placed = (
        (rows,) * 7 + (P(),) * 3 + (rows,) + (P(),) * 3 + (P("dp"),) * 2 + (rows,)
    )
    return jax.shard_map(
        shards,
        mesh=mesh,
        in_specs=placed,
        out_specs=rows,
        check_vma=False,
    )
```

```python
import functools

import jax
import jax.numpy as jnp
from jax import lax
from jax.experimental import pallas as pl
from jax.experimental.pallas import tpu as pltpu
from jax.sharding import PartitionSpec as P

eps_norm = 1e-06
f32 = jnp.float32
bf16 = jnp.bfloat16


def nt_dot(a, b):
    return lax.dot_general(a, b, (((1,), (1,)), ((), ())), preferred_element_type=f32)


def mixer_kernel(
    hidden_hbm,
    query_hbm,
    key_hbm,
    value_hbm,
    gate_hbm,
    decay_in_hbm,
    beta_in_hbm,
    decay_log_hbm,
    step_bias_hbm,
    norm_gain_hbm,
    post_gain_hbm,
    ids_hbm,
    state_hbm,
    proj_hbm,
    routed_ref,
    middle_ref,
    hidden_ref,
    query_ref,
    key_ref,
    value_ref,
    gate_ref,
    decay_in_ref,
    beta_in_ref,
    decay_log_ref,
    step_bias_ref,
    norm_gain_ref,
    post_gain_ref,
    ids_ref,
    state_buf,
    proj_buf,
    left_buf,
    right_buf,
    small_sem,
    state_sem,
    proj_sem,
):
    rows = query_ref.shape[0]
    value_heads, key_size, value_size = state_hbm.shape[1:]
    key_heads = query_ref.shape[2] // key_size
    share = value_heads // key_heads
    span = share * value_size
    chunks = proj_sem.shape[0]
    cut = proj_hbm.shape[0] // 2

    groups = state_sem.shape[0]
    group = key_heads // groups

    def state_copy(c):
        part = pl.ds(c * group * share, group * share)
        return pltpu.make_async_copy(
            state_hbm.at[:, part], state_buf.at[:, part], state_sem.at[c]
        )

    def proj_copy(c):
        part = pl.ds(c * cut, cut)
        return pltpu.make_async_copy(proj_hbm.at[part], proj_buf.at[part], proj_sem.at[c])

    pairs = (
        (key_hbm, key_ref),
        (query_hbm, query_ref),
        (decay_log_hbm, decay_log_ref),
        (step_bias_hbm, step_bias_ref),
        (decay_in_hbm, decay_in_ref),
        (beta_in_hbm, beta_in_ref),
        (norm_gain_hbm, norm_gain_ref),
        (value_hbm, value_ref),
        (gate_hbm, gate_ref),
        (ids_hbm, ids_ref),
        (hidden_hbm, hidden_ref),
        (post_gain_hbm, post_gain_ref),
    )
    small = [pltpu.make_async_copy(a, b, small_sem.at[i]) for i, (a, b) in enumerate(pairs)]
    early, late = small[:9], small[9:]
    for copy in early[:2]:
        copy.start()
    state_copy(0).start()
    for copy in early[2:]:
        copy.start()
    for c in range(1, groups):
        state_copy(c).start()
    for copy in late:
        copy.start()
    for c in range(chunks):
        proj_copy(c).start()
    for copy in early:
        copy.wait()

    query_all = query_ref[...].astype(f32)
    key_all = key_ref[...].astype(f32)
    value_all = value_ref[...].astype(f32)
    gate_all = gate_ref[...].astype(f32)
    decay_in = decay_in_ref[...].astype(f32)
    beta_in = beta_in_ref[...].astype(f32)
    rate = -jnp.exp(decay_log_ref[...].reshape(1, value_heads))
    bias = step_bias_ref[...].reshape(1, value_heads)
    decays, betas = [], []
    for p in range(2):
        decays.append(jnp.exp(rate * jax.nn.softplus(decay_in[:, p, :] + bias)))
        betas.append(1.0 / (1.0 + jnp.exp(-beta_in[:, p, :])))
    gain = norm_gain_ref[...].reshape(1, value_size)

    def joined(lists):
        return jnp.concatenate([jnp.concatenate(m, axis=-1) for m in lists], axis=0).astype(bf16)

    half = value_heads // 2
    mixed = [[], []]
    total = None
    for h in range(key_heads):
        if h == key_heads // 2:
            for copy in late:
                copy.wait()
            tokens, extra = 2 * rows, routed_ref.shape[1] - proj_hbm.shape[1]
            ids = jnp.concatenate([ids_ref[:, p, :] for p in range(2)], axis=0)
            lane = lax.broadcasted_iota(jnp.int32, (tokens, extra), 1)
            chosen = jnp.zeros((tokens, extra), f32)
            for k in range(ids.shape[1]):
                chosen = chosen + (ids[:, k : k + 1] == lane).astype(f32)
            routed_ref[:, -extra:] = chosen.astype(bf16)
        lanes = slice(h * key_size, (h + 1) * key_size)
        keys, queries = [], []
        for p in range(2):
            k = key_all[:, p, lanes]
            q = query_all[:, p, lanes]
            keys.append(k * lax.rsqrt(jnp.sum(k * k, axis=-1, keepdims=True) + eps_norm))
            queries.append(
                q
                * lax.rsqrt(jnp.sum(q * q, axis=-1, keepdims=True) + eps_norm)
                * key_size ** (-0.5)
            )
        vectors = (keys[0], queries[0], keys[1], queries[1])
        for j, v in enumerate(vectors):
            high = v.astype(bf16).astype(f32)
            left_buf[h, pl.ds(2 * j, rows, stride=8), :] = high
            left_buf[h, pl.ds(2 * j + 1, rows, stride=8), :] = v - high
        key_key = jnp.sum(keys[0] * keys[1], axis=-1, keepdims=True)
        key_query00 = jnp.sum(keys[0] * queries[0], axis=-1, keepdims=True)
        key_query01 = jnp.sum(keys[0] * queries[1], axis=-1, keepdims=True)
        key_query11 = jnp.sum(keys[1] * queries[1], axis=-1, keepdims=True)

        if h % group == 0:
            state_copy(h // group).wait()
            if h == key_heads - group:
                proj_copy(0).wait()
                total = jnp.dot(
                    joined([m[:half] for m in mixed]), proj_buf[:cut, :], preferred_element_type=f32
                )
        for r in range(rows):
            left = left_buf[h, r * 8 : (r + 1) * 8, :].astype(bf16)
            right = jnp.concatenate([state_buf[r, h * share + i] for i in range(share)], axis=-1)
            out = jnp.dot(left, right, preferred_element_type=f32)
            for i in range(share):
                right_buf[h, i, r * 8 : (r + 1) * 8, :] = out[:, i * value_size : (i + 1) * value_size]

        for i in range(share):
            n = h * share + i
            heads = slice(n * value_size, (n + 1) * value_size)
            part = [
                right_buf[h, i, pl.ds(2 * j, rows, stride=8), :]
                + right_buf[h, i, pl.ds(2 * j + 1, rows, stride=8), :]
                for j in range(4)
            ]
            d0, d1 = decays[0][:, n : n + 1], decays[1][:, n : n + 1]
            b0, b1 = betas[0][:, n : n + 1], betas[1][:, n : n + 1]
            u0 = b0 * (value_all[:, 0, heads] - d0 * part[0])
            o0 = d0 * part[1] + key_query00 * u0
            u1 = b1 * (value_all[:, 1, heads] - d1 * (d0 * part[2] + key_key * u0))
            o1 = d1 * (d0 * part[3] + key_query01 * u0) + key_query11 * u1
            for p, o in enumerate((o0, o1)):
                g = gate_all[:, p, heads]
                mean = jnp.mean(o * o, axis=-1, keepdims=True)
                mixed[p].append(
                    o * lax.rsqrt(mean + eps_norm) * gain * (g / (1.0 + jnp.exp(-g)))
                )

    hidden = hidden_ref[...].astype(f32)
    total = total + jnp.concatenate([hidden[:, p, :] for p in range(2)], axis=0)
    proj_copy(1).wait()
    total = total + jnp.dot(
        joined([m[half:] for m in mixed]), proj_buf[cut:, :], preferred_element_type=f32
    )
    middle = total.astype(bf16)
    middle_ref[...] = middle
    wide = middle.astype(f32)
    routed = (
        wide
        * lax.rsqrt(jnp.mean(wide * wide, axis=-1, keepdims=True) + eps_norm)
        * post_gain_ref[...].reshape(1, wide.shape[1])
    ).astype(bf16)
    routed_ref[:, : routed.shape[1]] = routed


def choice_place(experts, piece):
    per = max(1, 128 // experts)
    return piece // per, piece % per * experts


def column_kernel(experts, *refs):
    out_ref = refs[-1]
    pieces = refs[:-1]
    tokens = pieces[0].shape[0]
    width = pieces[0].shape[1] - 128
    column = tokens * len(pieces)
    for i, ref in enumerate(pieces):
        for j in range(width // 128):
            first = j * column + i * tokens
            out_ref[first : first + tokens, :] = ref[:, j * 128 : (j + 1) * 128]
    groups = {}
    for i, ref in enumerate(pieces):
        group, start = choice_place(experts, i)
        choices = ref[:, width:].astype(f32)
        if start:
            choices = pltpu.roll(choices, start, 1)
        groups[group] = choices + groups.get(group, 0.0)
    first = column * (width // 128)
    for group, choices in groups.items():
        out_ref[first + group * tokens : first + (group + 1) * tokens, :] = choices.astype(bf16)


def expert_kernel(tokens, count, *refs):
    blocks = refs[:count]
    router, up_own, down_own, up_other, down_other = refs[count : count + 5]
    outs = refs[count + 5 :]
    rows, width = outs[0].shape
    hidden_units = down_own.shape[1]
    me = lax.axis_index("dp")
    experts = router.shape[0]
    blocks_rows, blocks_chosen = [], []
    for block in blocks:
        parts = [block[j * rows : (j + 1) * rows, :] for j in range(width // 128)]
        blocks_rows.append(jnp.concatenate(parts, axis=-1))
        for i in range(rows // tokens):
            group, start = choice_place(experts, i)
            first = rows * (width // 128) + group * tokens
            choices = block[first : first + tokens, :].astype(f32)
            if start:
                choices = pltpu.roll(choices, 128 - start, 1)
            blocks_chosen.append(choices[:, :experts])
    x = jnp.concatenate(blocks_rows, axis=0)
    chosen = jnp.concatenate(blocks_chosen, axis=0) > 0.0
    raised = jnp.where(chosen, jnp.exp(nt_dot(x, router[...])), 0.0)
    whole = jnp.sum(raised, axis=-1, keepdims=True)
    lane = lax.broadcasted_iota(jnp.int32, raised.shape, 1)
    total = None
    for up_ref, down_ref, e in ((up_own, down_own, me), (up_other, down_other, me ^ 1)):
        both = jnp.dot(x, up_ref[0], preferred_element_type=f32)
        g = both[:, :hidden_units]
        activated = (g / (1.0 + jnp.exp(-g)) * both[:, hidden_units:]).astype(bf16)
        result = jnp.dot(activated, down_ref[0], preferred_element_type=f32).astype(bf16)
        share = jnp.sum(jnp.where(lane == e, raised, 0.0), axis=-1, keepdims=True) / whole
        part = share * result.astype(f32)
        total = part if total is None else total + part
    for i, out in enumerate(outs):
        out[...] = total[i * rows : (i + 1) * rows].astype(out.dtype)


def column_sum_kernel(tokens, *refs):
    own_ref = refs[0]
    count = (own_ref.shape[0] // tokens)
    outs = refs[-count:]
    total = own_ref[...]
    for ref in refs[1:-count]:
        total = total + ref[...].astype(f32)
    for i, out in enumerate(outs):
        out[...] = total[i * tokens : (i + 1) * tokens].astype(out.dtype)


def final_kernel(*refs):
    out_ref = refs[-1]
    rows = out_ref.shape[0]
    total = refs[0][...].astype(f32) + refs[1][...]
    for ref in refs[2:-1]:
        total = total + ref[...].astype(f32)
    total = total.astype(bf16)
    for p in range(2):
        out_ref[:, p, :] = total[p * rows : (p + 1) * rows]


def chip_masks(device_count):
    bits = device_count.bit_length() - 2
    low = bits // 2
    near = [m << 1 for m in range(1, 1 << low)]
    far = [m << (1 + low) for m in range(1, 1 << (bits - low))]
    if len(near) != len(far):
        return list(zip(far, far)), list(zip(near, near))
    turned = [near[1], near[0], *near[2:]]
    return list(zip(far, near)), list(zip(turned, far))


def hop(x, masks):
    count = lax.axis_size("dp")
    return lax.ppermute(x, "dp", [(i, i ^ masks[i % 2]) for i in range(count)])


def vmem(count):
    return [pl.BlockSpec(memory_space=pltpu.VMEM)] * count


def shards(
    hidden_in,
    query_in,
    key_in,
    value_in,
    gate_in,
    decay_in,
    beta_in,
    decay_log,
    step_bias,
    norm_gain,
    state_in,
    out_proj,
    post_gain,
    router_weight,
    expert_gate_up,
    expert_down,
    expert_ids,
):
    device_count = lax.axis_size("dp")
    expert_total = expert_gate_up.shape[0] * device_count
    row_count, _, model_width = hidden_in.shape
    value_heads, key_size, value_size = state_in.shape[1:]
    key_heads = query_in.shape[2] // key_size
    share = value_heads // key_heads
    token_count = row_count * 2
    sent_width = model_width + 128
    first, second = chip_masks(device_count)
    chunks = 2
    params = pltpu.CompilerParams(vmem_limit_bytes=48 * 1024 * 1024)
    operands = (
        hidden_in,
        query_in,
        key_in,
        value_in,
        gate_in,
        decay_in,
        beta_in,
        decay_log,
        step_bias,
        norm_gain,
        post_gain,
        expert_ids,
        state_in,
        out_proj,
    )
    operands = [pltpu.with_memory_space_constraint(x, pltpu.HBM) for x in operands]
    up_other, down_other = hop(expert_gate_up, (1, 1)), hop(expert_down, (1, 1))
    routed, middle = pl.pallas_call(
        mixer_kernel,
        out_shape=(
            jax.ShapeDtypeStruct((token_count, sent_width), bf16),
            jax.ShapeDtypeStruct((token_count, model_width), bf16),
        ),
        in_specs=[pl.BlockSpec(memory_space=pltpu.HBM)] * len(operands),
        out_specs=tuple(vmem(2)),
        scratch_shapes=[pltpu.VMEM(x.shape, x.dtype) for x in operands[:12]]
        + [
            pltpu.VMEM(state_in.shape, bf16),
            pltpu.VMEM(out_proj.shape, bf16),
            pltpu.VMEM((key_heads, 8 * row_count, key_size), f32),
            pltpu.VMEM((key_heads, share, 8 * row_count, value_size), f32),
            pltpu.SemaphoreType.DMA((12,)),
            pltpu.SemaphoreType.DMA((key_heads // 4,)),
            pltpu.SemaphoreType.DMA((chunks,)),
        ],
        compiler_params=params,
        name="mixer",
    )(*operands)

    def local(body, name, outs, *args):
        return pl.pallas_call(
            body,
            out_shape=tuple(jax.ShapeDtypeStruct(*o) for o in outs),
            in_specs=vmem(len(args)),
            out_specs=tuple(vmem(len(outs))),
            compiler_params=params,
            name=name,
        )(*args)

    weights = (router_weight.T, expert_gate_up, expert_down, up_other, down_other)
    column_rows = token_count * (len(first) + 1)
    groups = choice_place(expert_total, len(first))[0] + 1
    column_size = column_rows * (model_width // 128) + groups * token_count
    pieces = [hop(routed, m) for m in first]
    (column,) = local(
        functools.partial(column_kernel, expert_total),
        "column",
        [((column_size, 128), bf16)],
        routed,
        *pieces,
    )
    columns = [hop(column, m) for m in second]
    (own,) = local(
        functools.partial(expert_kernel, token_count, 1),
        "own_experts",
        [((column_rows, model_width), f32)],
        column,
        *weights,
    )
    results = local(
        functools.partial(expert_kernel, token_count, len(second)),
        "experts",
        [((column_rows, model_width), bf16)] * len(second),
        *columns,
        *weights,
    )
    back = [hop(r, m) for r, m in zip(results[::-1], second[::-1])]
    mine, *others = local(
        functools.partial(column_sum_kernel, token_count),
        "column_sum",
        [((token_count, model_width), f32)] + [((token_count, model_width), bf16)] * len(first),
        own,
        *back,
    )
    home = [hop(r, m) for r, m in zip(others[::-1], first[::-1])]
    (out,) = local(final_kernel, "final", [(hidden_in.shape, bf16)], middle, mine, *home)
    return out


def solution(mesh):
    rows = P(("groups", "dp"))
    placed = (
        (rows,) * 7 + (P(),) * 3 + (rows,) + (P(),) * 3 + (P("dp"),) * 2 + (rows,)
    )
    return jax.shard_map(
        shards,
        mesh=mesh,
        in_specs=placed,
        out_specs=rows,
        check_vma=False,
    )
```
